256 devices in a mesh: ka: 8 (over z_lo, x), ta: 32 (over y, z_hi, core).
Axes of the slice: x: 4, y: 4, z: 8 (z_hi: 4, z_lo: 2; z = z_hi * 2 + z_lo), core: 2. Of those that a mesh axis runs over, the one named last changes fastest.
Arguments:
- amplitudes: float32 [6144, 6144], P('ta', 'ka'), may hold values from -6 to 6
- driving: float32 [6144, 6144], P('ta', 'ka'), may hold values from -24 to 24
- cycle_ints: bfloat16 [6144, 6144], P('ka', 'ta'), may hold values from -0.078125 to 0.078125
- occ_irrep: int32 [128], replicated, may hold values from 0 to 3
- vir_irrep: int32 [1536], replicated, may hold values from 0 to 3
- occ_energy: float32 [128], replicated, may hold values from -2 to -0.5
- vir_energy: float32 [1536], replicated, may hold values from 0.3 to 3
- slab: int32 [4], replicated, may hold values from 0 to 127
Outputs:
- updated: float32 [6144, 6144], P('ta', 'ka')
The draws below stay inside these ranges and needn't reach their ends.
Inputs may be any that keep to these rules, and one draw needn't show every extreme that they name: `slab`: slab positions may name the same occupied orbital more than once.
All inputs are finite; a program needn't handle non-finite values.
Results may differ from the reference program's by a relative error of at most 0.00048.
Values may be sent and summed in bfloat16 or wider, within the bound.
A program may use at most 64 MiB of HBM per device.

```python
import jax
import jax.numpy as jnp

VIRT = 1536
NOCC = 128
SLAB = 4
ITERS = 2
NC = 6144
RB = 24
N_KA = 8
N_TA = 32


def set_ends(entries, own_key, least, largest):
    spot = [jax.random.randint(jax.random.fold_in(own_key, axis), (), 0, length) for axis, length in enumerate(entries.shape)]
    main_axis = entries.shape.index(max(entries.shape))
    next_to = spot[:main_axis] + [(spot[main_axis] + 1) % entries.shape[main_axis]] + spot[main_axis + 1:]
    return entries.at[tuple(spot)].set(least).at[tuple(next_to)].set(largest)


def shard_levels(own_key, dims, split, low, top_value):
    level = 1.0
    for position, blocks in split:
        steps = jax.random.uniform(jax.random.fold_in(jax.random.fold_in(own_key, 6), position), (blocks,), jnp.float32, low / len(split), top_value / len(split))
        level = level * jnp.repeat(jnp.exp(steps), dims[position] // blocks).reshape((-1,) + (1,) * (len(dims) - 1 - position))
    return level


def noise(stream_key, extent, spread, reach, cuts=(), held_as=jnp.bfloat16):
    factor_of = shard_levels(stream_key, extent, cuts, -0.22, 0.18) if cuts else 1.0
    entries = jax.random.normal(stream_key, extent, jnp.float32) * spread * factor_of
    return jnp.minimum(jnp.maximum(entries, -reach), reach).astype(held_as)


def setup_inputs(seed: int = 0) -> dict:
    keys = jax.random.split(jax.random.key(seed), 9)
    return {
        "amplitudes": noise(keys[0], (NC, NC), 1.0, 6.0, ((0, 32), (1, 8)), jnp.float32),
        "driving": noise(keys[1], (NC, NC), 4.0, 24.0, ((0, 32), (1, 8)), jnp.float32),
        "cycle_ints": noise(keys[2], (NC, NC), NC ** -0.5, 0.078125, ((0, 8), (1, 32))),
        "occ_irrep": set_ends(jax.random.randint(keys[3], (NOCC,), 0, 4), jax.random.fold_in(keys[3], 1), 0, 3).astype(jnp.int32),
        "vir_irrep": set_ends(jax.random.randint(keys[4], (VIRT,), 0, 4), jax.random.fold_in(keys[4], 1), 0, 3).astype(jnp.int32),
        "occ_energy": jnp.clip(jax.random.uniform(keys[5], (NOCC,), jnp.float32, -2.0, -0.5), -2.0, -0.5),
        "vir_energy": jnp.clip(jax.random.uniform(keys[6], (VIRT,), jnp.float32, 0.3, 3.0), 0.3, 3.0),
        "slab": set_ends(jax.random.randint(keys[7], (SLAB,), 0, NOCC), jax.random.fold_in(keys[7], 1), 0, NOCC - 1).astype(jnp.int32),
    }


def labels(occ_irrep, vir_irrep, occ_energy, vir_energy, slab):
    picked = slab[:, None] == jnp.arange(occ_irrep.shape[0], dtype=jnp.int32)[None, :]
    slab_irrep = jnp.sum(jnp.where(picked, occ_irrep[None, :], 0), axis=1).astype(jnp.int32)
    slab_energy = jnp.sum(jnp.where(picked, occ_energy[None, :], 0.0), axis=1)
    irrep = jnp.bitwise_xor(slab_irrep[:, None], vir_irrep[None, :]).reshape(-1)
    energy = (vir_energy[None, :] - slab_energy[:, None]).reshape(-1)
    return irrep, energy


def cols_natural(matrix):
    return matrix.reshape(NC, N_KA, N_TA, RB).transpose(0, 2, 1, 3).reshape(NC, NC)


def cols_stored(matrix):
    return matrix.reshape(NC, N_TA, N_KA, RB).transpose(0, 2, 1, 3).reshape(NC, NC)


def rows_natural(matrix):
    return matrix.reshape(N_KA, N_TA, RB, NC).transpose(1, 0, 2, 3).reshape(NC, NC)


def reference(amplitudes, driving, cycle_ints, occ_irrep, vir_irrep, occ_energy, vir_energy, slab):
    irrep, energy = labels(occ_irrep, vir_irrep, occ_energy, vir_energy, slab)
    mask = irrep[:, None] == irrep[None, :]
    denom = energy[:, None] + energy[None, :]
    current = cols_natural(amplitudes)
    source = cols_natural(driving)
    integrals = rows_natural(cycle_ints)
    for step in range(ITERS):
        cycle = jnp.dot(current.astype(jnp.bfloat16), integrals, preferred_element_type=jnp.float32)
        total = source + cycle + cycle.T
        current = jnp.where(mask, -total / denom, 0.0)
    return cols_stored(current)
```

```python
import functools

import jax
import jax.numpy as jnp
from jax import lax
from jax.experimental import pallas as pl
from jax.experimental.pallas import tpu as pltpu
from jax.sharding import PartitionSpec as P

ITERS = 2
MESH = pl.DeviceIdType.MESH
NT = (((1,), (1,)), ((), ()))


def labels(occ_irrep, vir_irrep, occ_energy, vir_energy, slab):
    picked = slab[:, None] == jnp.arange(occ_irrep.shape[0], dtype=jnp.int32)[None, :]
    slab_irrep = jnp.sum(jnp.where(picked, occ_irrep[None, :], 0), axis=1)
    slab_energy = jnp.sum(jnp.where(picked, occ_energy[None, :], 0.0), axis=1)
    irrep = jnp.bitwise_xor(slab_irrep[:, None], vir_irrep[None, :]).reshape(-1)
    energy = (vir_energy[None, :] - slab_energy[:, None]).reshape(-1)
    return (irrep, energy)


def kernel(amp, drv, rloc, rowe, cole, rowi, coli, out,
           rpair, rsend, rt, ball, ct, u, xs, m,
           p_s, p_r, a_s, a_r, b_s, b_r, z_s, y_s, c_s, r_r, c_r, u_s, u_r, m_s, m_r):
    s = lax.axis_index("ka")
    t = lax.axis_index("ta")
    zlo, x = s // 4, s % 4
    y, zhi, core = t // 8, (t // 2) % 4, t % 2
    j = t // 2
    other = 1 - core

    def dev_t(yy, zz, cc):
        return (s, (yy * 4 + zz) * 2 + cc)

    zpart = ((1 - zlo) * 4 + x, t)
    cpart = dev_t(y, zhi, other)
    kpeers = [(s + d) % 8 for d in range(1, 8)]
    greet = [(q, t) for q in kpeers] + [cpart]
    greet += [dev_t(y, (zhi + d) % 4, core) for d in (1, 2, 3)]
    greet += [dev_t((y + d) % 4, zhi, core) for d in (1, 2, 3)]
    barrier = pltpu.get_barrier_semaphore()
    for peer in greet:
        pl.semaphore_signal(barrier, inc=1, device_id=peer, device_id_type=MESH)
    pl.semaphore_wait(barrier, len(greet))

    pending = []

    def send(src, dst, ss, rs, peer):
        copy = pltpu.make_async_remote_copy(
            src_ref=src, dst_ref=dst, send_sem=ss, recv_sem=rs, device_id=peer, device_id_type=MESH)
        copy.start()
        pending.append(copy)

    def arrived(dst, rs):
        pltpu.make_async_remote_copy(
            src_ref=dst, dst_ref=dst, send_sem=p_s, recv_sem=rs, device_id=cpart, device_id_type=MESH).wait_recv()

    send(rloc, rpair, p_s, p_r, cpart)

    def spread_b(it):
        mine = ball.at[it, s]
        send(mine, mine, b_s.at[it, 0], b_r.at[it, s], zpart)
        for d in (1, 3, 2):
            send(mine, mine, b_s.at[it, d], b_r.at[it, s], (zlo * 4 + (x + d) % 4, t))

    def relay_b(it):
        q = (1 - zlo) * 4 + x
        arrived(ball.at[it, q], b_r.at[it, q])
        for d in (1, 3, 2):
            send(ball.at[it, q], ball.at[it, q], b_s.at[it, 3 + d], b_r.at[it, q], (zlo * 4 + (x + d) % 4, t))

    def await_b(it):
        for z in (0, 1):
            for d in (1, 3, 2):
                q = (zlo + z) % 2 * 4 + (x + d) % 4
                arrived(ball.at[it, q], b_r.at[it, q])

    ball[0, s] = amp[...].astype(jnp.bfloat16)
    spread_b(0)

    arrived(rpair, p_r)
    own_first = core == 0
    for q in range(8):
        a = rloc[q].astype(jnp.float32)
        b = rpair[q].astype(jnp.float32)
        both = jnp.concatenate([jnp.where(own_first, a, b), jnp.where(own_first, b, a)], axis=0).astype(jnp.bfloat16)
        rsend[q] = jnp.where(own_first, both[:, :384], both[:, 384:])
    base = pl.multiple_of(core * 3072, 3072)

    def kslot(q):
        return pl.ds(pl.multiple_of(base + q * 384, 384), 384)

    rt[j, :, kslot(s)] = rsend[s]
    for d in range(1, 8):
        q = (s + d) % 8
        send(rsend.at[q], rt.at[j, :, kslot(s)], a_s.at[d], a_r.at[s], (q, t))
    for d in range(1, 8):
        q = (s + d) % 8
        arrived(rt.at[j, :, kslot(q)], a_r.at[q])

    def piece(jj, p, c=None):
        start = (core if c is None else c) * 3072 + p * 1536
        return rt.at[jj, :, pl.ds(pl.multiple_of(start, 1536), 1536)]

    def to_y(i, jj):
        for p in (0, 1):
            send(piece(jj, p), piece(jj, p), y_s.at[i, 0, p], r_r.at[jj, p], dev_t((y + 1) % 4, zhi, core))
            send(piece(jj, p), piece(jj, p), y_s.at[i, 1, p], r_r.at[jj, p], dev_t((y + 3) % 4, zhi, core))

    def to_core(i, jj, p):
        send(piece(jj, p), piece(jj, p), c_s.at[i, p], c_r.at[jj, p], cpart)

    for p in (0, 1):
        to_core(0, j, p)
    to_y(0, j)
    for p in (0, 1):
        for d in (1, 3, 2):
            send(piece(j, p), piece(j, p), z_s.at[d, p], r_r.at[j, p], dev_t(y, (zhi + d) % 4, core))
    relay_b(0)
    for i, d in ((1, 1), (2, 3), (3, 2)):
        jj = y * 4 + (zhi + d) % 4
        for p in (0, 1):
            arrived(piece(jj, p), r_r.at[jj, p])
            to_core(i, jj, p)
        to_y(i, jj)

    def group(it, yy):
        def step(k, acc):
            h, q = k // 8, k % 8
            left = rt[pl.ds(yy * 4, 4), :, pl.ds(pl.multiple_of(k * 384, 384), 384)].reshape(192, 384)
            right = ball[it, q, :, pl.ds(pl.multiple_of(h * 384, 384), 384)]
            return acc + lax.dot_general(left, right, NT, preferred_element_type=jnp.float32)
        acc = lax.fori_loop(0, 16, step, jnp.zeros((192, 192), jnp.float32))
        ct[it, pl.ds(yy * 8, 8)] = acc.reshape(8, 24, 192)

    def mirror_a(it, g, yy):
        for e in range(8):
            tt = yy * 8 + (t + e) % 8
            k = g * 8 + e
            if k == 0:
                u[it, t] = ct[it, t]
            else:
                send(ct.at[it, tt], u.at[it, t], u_s.at[it, k], u_r.at[it, t], (s, tt))

    def mirror_b(it):
        for g in range(4):
            for e in range(8):
                if g + e:
                    tt = (y + g) % 4 * 8 + (t + e) % 8
                    arrived(u.at[it, tt], u_r.at[it, tt])
        for q in range(8):
            xs[it, q] = jnp.concatenate([u[it, i, :, q * 24:(q + 1) * 24] for i in range(32)], axis=1)
        m[it, s] = xs[it, s]
        for d in range(1, 8):
            q = (s + d) % 8
            send(xs.at[it, q], m.at[it, s], m_s.at[it, d], m_r.at[it, s], (q, t))

    def total(it):
        c = jnp.concatenate([ct[it].reshape(768, 192), jnp.zeros((768, 64), jnp.float32)], axis=1).T[:192]
        for d in range(1, 8):
            q = (s + d) % 8
            arrived(m.at[it, q], m_r.at[it, q])
        return drv[...] + c + m[it].reshape(192, 768)

    await_b(0)
    for g, d in enumerate((0, 1, 3, 2)):
        yy = (y + d) % 4
        for i, e in enumerate((0, 1, 3, 2)):
            jj = yy * 4 + (zhi + e) % 4
            for p in (0, 1):
                if g:
                    arrived(piece(jj, p), r_r.at[jj, p])
                    to_core(g * 4 + i, jj, p)
                if (g, p) == (1, 1):
                    send(piece(jj, p), piece(jj, p), y_s.at[i, 2, p], r_r.at[jj, p], dev_t((y + 3) % 4, zhi, core))
                if (g, p) == (2, 0):
                    send(piece(jj, p), piece(jj, p), y_s.at[i, 2, p], r_r.at[jj, p], dev_t((y + 1) % 4, zhi, core))
        for i, e in enumerate((0, 1, 3, 2)):
            jj = yy * 4 + (zhi + e) % 4
            for p in (0, 1):
                arrived(piece(jj, p, other), c_r.at[jj, p])
        group(0, yy)
        mirror_a(0, g, yy)
    mirror_b(0)
    tot = total(0)
    keep = rowi[...] == coli[...]
    nxt = jnp.where(keep, -tot / (rowe[...] + cole[...]), 0.0)
    ball[1, s] = nxt.astype(jnp.bfloat16)
    spread_b(1)
    relay_b(1)
    await_b(1)
    for g, d in enumerate((0, 1, 3, 2)):
        yy = (y + d) % 4
        group(1, yy)
        mirror_a(1, g, yy)
    mirror_b(1)
    out[...] = total(1)
    for copy in pending:
        copy.wait_send()


def local(amplitudes, driving, cycle_ints, occ_irrep, vir_irrep, occ_energy, vir_energy, slab):
    n_ka = lax.axis_size("ka")
    n_ta = lax.axis_size("ta")
    rows, cols = amplitudes.shape
    block = rows // n_ka
    t, s = lax.axis_index("ta"), lax.axis_index("ka")
    irrep, energy = labels(occ_irrep, vir_irrep, occ_energy, vir_energy, slab)
    pick = functools.partial(lax.dynamic_index_in_dim, keepdims=False)
    rowi = pick(irrep.reshape(n_ta, rows), t, 0).reshape(rows, 1)
    rowe = pick(energy.reshape(n_ta, rows), t, 0).reshape(rows, 1)
    coli = pick(irrep.reshape(n_ta, n_ka, block), s, 1).reshape(1, cols)
    cole = pick(energy.reshape(n_ta, n_ka, block), s, 1).reshape(1, cols)
    rloc = cycle_ints.T.reshape(n_ka, block, cols)
    f32, bf16 = jnp.float32, jnp.bfloat16
    dma = pltpu.SemaphoreType.DMA
    tot = pl.pallas_call(
        kernel,
        out_shape=jax.ShapeDtypeStruct((rows, cols), f32),
        in_specs=[pl.BlockSpec(memory_space=pltpu.VMEM)] * 7,
        out_specs=pl.BlockSpec(memory_space=pltpu.VMEM),
        scratch_shapes=[
            pltpu.VMEM((8, 24, 768), bf16),
            pltpu.VMEM((8, 48, 384), bf16),
            pltpu.VMEM((16, 48, 6144), bf16),
            pltpu.VMEM((2, 8, 192, 768), bf16),
            pltpu.VMEM((2, 32, 24, 192), f32),
            pltpu.VMEM((2, 32, 24, 192), f32),
            pltpu.VMEM((2, 8, 24, 768), f32),
            pltpu.VMEM((2, 8, 24, 768), f32),
            dma, dma,
            dma((8,)), dma((8,)),
            dma((2, 7)), dma((2, 8)),
            dma((4, 2)), dma((4, 3, 2)), dma((16, 2)), dma((16, 2)), dma((16, 2)),
            dma((2, 32)), dma((2, 32)),
            dma((2, 8)), dma((2, 8)),
        ],
        compiler_params=pltpu.CompilerParams(
            collective_id=0, has_side_effects=True, vmem_limit_bytes=48 * 2**20),
        cost_estimate=pl.CostEstimate(flops=2 * 2 * 192 * 768 * 6144, bytes_accessed=3 * 2**20, transcendentals=0),
    )(amplitudes, driving, rloc, rowe, cole, rowi, coli)
    return jnp.where(rowi == coli, -tot / (rowe + cole), 0.0)


def solution(mesh):
    in_specs = (P("ta", "ka"), P("ta", "ka"), P("ka", "ta"), P(), P(), P(), P(), P())
    return jax.shard_map(local, mesh=mesh, in_specs=in_specs, out_specs=P("ta", "ka"), check_vma=False)
```

```python
import jax
import jax.numpy as jnp
from jax import lax
from jax.experimental import pallas as pl
from jax.experimental.pallas import tpu as pltpu
from jax.sharding import PartitionSpec as P

MESH = pl.DeviceIdType.MESH
NT = (((1,), (1,)), ((), ()))
F32, BF16 = jnp.float32, jnp.bfloat16


PIECES = ((0, 1280), (1280, 1280), (2560, 512))


def kernel(amp_h, drv_h, rloc_h, vire, viri, occe, occi, slab, out,
           amp, drv, rloc, rpair, rsend, rt, ball, bn, ct, cp, pk, u, xs, m, ch,
           l_s, s_s, p_r, a_r, b_r, r_r, c_r, cp_r, u_r, m_r):
    s = lax.axis_index("ka")
    t = lax.axis_index("ta")
    zlo, x = s // 4, s % 4
    y, zhi, core = t // 8, (t // 2) % 4, t % 2
    j = t // 2
    other = 1 - core

    loads = [pltpu.make_async_copy(rloc_h, rloc, l_s.at[0]),
             pltpu.make_async_copy(amp_h, amp, l_s.at[1]),
             pltpu.make_async_copy(drv_h, drv, l_s.at[2])]
    for copy in loads:
        copy.start()

    def dev(dy, dz):
        return (s, ((y + dy) % 4 * 4 + (zhi + dz) % 4) * 2 + core)

    zp = (1 - zlo) * 4 + x
    cpart = (s, j * 2 + other)
    greet = [((s + d) % 8, t) for d in range(1, 8)] + [cpart]
    greet += [dev(0, d) for d in (1, 2, 3)] + [dev(d, 0) for d in (1, 2, 3)]
    barrier = pltpu.get_barrier_semaphore()
    for peer in greet:
        pl.semaphore_signal(barrier, inc=1, device_id=peer, device_id_type=MESH)
    pl.semaphore_wait(barrier, len(greet))

    pending = []

    def send(src, dst, rs, peer):
        copy = pltpu.make_async_remote_copy(
            src_ref=src, dst_ref=dst, send_sem=s_s.at[len(pending)], recv_sem=rs, device_id=peer, device_id_type=MESH)
        copy.start()
        pending.append(copy)

    def arrived(dst, rs):
        pltpu.make_async_remote_copy(
            src_ref=dst, dst_ref=dst, send_sem=s_s.at[0], recv_sem=rs, device_id=cpart, device_id_type=MESH).wait_recv()

    loads[0].wait()
    send(rloc, rpair, p_r, cpart)
    loads[1].wait()
    for k in range(3):
        ball[0, k, s] = amp[k * 64:k * 64 + 64].astype(BF16)
    arrived(rpair, p_r)
    own_first = core == 0
    for q in range(8):
        a = rloc[q].astype(F32)
        b = rpair[q].astype(F32)
        both = jnp.concatenate([jnp.where(own_first, a, b), jnp.where(own_first, b, a)], axis=0).astype(BF16)
        rsend[q] = jnp.where(own_first, both[:, :384], both[:, 384:])

    def kslot(q):
        return pl.ds(pl.multiple_of(core * 3072 + q * 384, 384), 384)

    for d in range(1, 8):
        q = (s + d) % 8
        send(rsend.at[q], rt.at[j, :, kslot(s)], a_r.at[s], (q, t))
    rt[j, :, kslot(s)] = rsend[s]

    hot = lax.broadcasted_iota(jnp.int32, (1, 128), 1)

    def slab_at(i):
        here = hot == slab[i]
        return (jnp.sum(jnp.where(here, occe[...], 0.0), axis=1, keepdims=True),
                jnp.sum(jnp.where(here, occi[...], 0), axis=1, keepdims=True))

    def tile_part(v):
        runs = [jnp.concatenate([v[:, i * 192 + q * 24:i * 192 + q * 24 + 24] for i in range(8)], axis=1) for q in range(8)]
        part = runs[0]
        for q in range(1, 8):
            part = jnp.where(s == q, runs[q], part)
        return part

    def row_part(v):
        part = v[:, :192]
        for i in range(1, 8):
            part = jnp.where(t % 8 == i, v[:, i * 192:i * 192 + 192], part)
        return part

    picked = [slab_at(i) for i in range(4)]
    vce, vci = tile_part(vire[...]), tile_part(viri[...])
    cole = jnp.concatenate([vce - picked[i][0] for i in range(4)], axis=1)
    coli = jnp.concatenate([jnp.bitwise_xor(vci, picked[i][1]) for i in range(4)], axis=1)
    rowe_v, rowi_v = slab_at(y)
    rowe_l = row_part(vire[...]) - rowe_v
    rowi_l = jnp.bitwise_xor(row_part(viri[...]), rowi_v).astype(F32)

    def stand(line):
        wide = jnp.concatenate([line, jnp.zeros((1, 64), F32)], axis=1)
        return jnp.broadcast_to(wide, (128, 256)).T[:192, :1]

    rowe = stand(rowe_l).reshape(8, 24, 1)
    rowi = stand(rowi_l).reshape(8, 24, 1)
    coli = coli.astype(F32)

    for d in range(1, 8):
        q = (s + d) % 8
        arrived(rt.at[j, :, kslot(q)], a_r.at[q])

    def piece(jj, p, c):
        start, size = PIECES[p]
        return rt.at[jj, :, pl.ds(pl.multiple_of(c * 3072 + start, 128), size)]

    def ahead(jj, p, peer):
        send(piece(jj, p, core), piece(jj, p, core), r_r.at[jj, p], peer)

    def to_core(jj, p):
        send(piece(jj, p, core), piece(jj, p, core), c_r.at[jj, p], cpart)

    def event(dy, dz, p):
        jj = (y + dy) % 4 * 4 + (zhi + dz) % 4
        arrived(piece(jj, p, core), r_r.at[jj, p])
        if p < 2:
            if dy == 0:
                if (dz, p) == (3, 0):
                    ahead(jj, p, dev(0, 1))
                if (dz, p) == (1, 1):
                    ahead(jj, p, dev(0, 3))
                ahead(jj, p, dev(1, 0))
                ahead(jj, p, dev(3, 0))
            if (dy, p) == (3, 0):
                ahead(jj, p, dev(1, 0))
            if (dy, p) == (1, 1):
                ahead(jj, p, dev(3, 0))
        elif dz == 0:
            for d in (1, 3, 2):
                ahead(jj, p, dev(0, d))
        to_core(jj, p)

    def bpart(it, k, q, h):
        return ball.at[it, k, q, h * 32:h * 32 + 32]

    def b_to(it, k, q, h, peer):
        send(bpart(it, k, q, h), bpart(it, k, q, h), b_r.at[it, k, q, h], (peer, t))

    def b_at(it, k, q, h):
        arrived(bpart(it, k, q, h), b_r.at[it, k, q, h])

    def round_x(d):
        return zlo * 4 + (x + d) % 4

    def spread_b(it, k):
        for h in (0, 1):
            b_to(it, k, s, h, zp)
        for h in (0, 1):
            b_to(it, k, s, h, round_x(1))
            b_to(it, k, s, h, round_x(3))

    def partner_b(it, k):
        for h in (0, 1):
            b_at(it, k, zp, h)
            b_to(it, k, zp, h, round_x(1))
            b_to(it, k, zp, h, round_x(3))

    def onward_b(it, k, z):
        left = (zlo + z) % 2 * 4 + (x + 3) % 4
        right = (zlo + z) % 2 * 4 + (x + 1) % 4
        b_at(it, k, left, 0)
        b_to(it, k, left, 0, round_x(1))
        b_at(it, k, right, 0)
        b_at(it, k, left, 1)
        b_at(it, k, right, 1)
        b_to(it, k, right, 1, round_x(3))

    def last_b(it, k):
        for z in (0, 1):
            for h in (0, 1):
                b_at(it, k, (zlo + z) % 2 * 4 + (x + 2) % 4, h)

    for p in (0, 1):
        ahead(j, p, dev(0, 1))
        ahead(j, p, dev(0, 3))
        ahead(j, p, dev(1, 0))
        ahead(j, p, dev(3, 0))
    for d in (1, 3, 2):
        ahead(j, 2, dev(d, 0))
    for k in range(3):
        spread_b(0, k)
    for p in (0, 1, 2):
        to_core(j, p)
    for p in (0, 1):
        for d in (3, 1):
            event(0, d, p)
            event(d, 0, p)
    for d in (1, 3, 2):
        ahead(j, 2, dev(0, d))
    for k in range(3):
        onward_b(0, k, 0)
    event(1, 0, 2)
    event(3, 0, 2)
    for p in (0, 1):
        event(0, 2, p)
        event(2, 0, p)
    event(2, 0, 2)
    for k in range(3):
        partner_b(0, k)
    for p in (0, 1):
        for dz in (3, 1):
            for dy in (3, 1):
                event(dy, dz, p)
    for k in range(3):
        onward_b(0, k, 1)
    for p in (0, 1):
        for dy in (3, 1):
            event(dy, 2, p)
    for p in (0, 1):
        for dz in (3, 1):
            event(2, dz, p)
    for dz in (1, 3, 2):
        for dy in (0, 1, 3, 2):
            event(dy, dz, 2)
    for p in (0, 1):
        event(2, 2, p)
    for k in range(3):
        last_b(0, k)
    for dy in (0, 1, 3, 2):
        for dz in (0, 1, 3, 2):
            jj = (y + dy) % 4 * 4 + (zhi + dz) % 4
            for p in (0, 1, 2):
                arrived(piece(jj, p, other), c_r.at[jj, p])

    def cycle(it, rhs):
        slabs = [(y + d) % 4 for d in (2, 1, 3, 0)]
        for yy in slabs:
            left = rt[pl.ds(yy * 4, 4)].reshape(192, 6144)
            acc = lax.dot_general(left, rhs(), NT, preferred_element_type=F32).reshape(4, 2, 24, 192)
            ct[it, 0, pl.ds(yy * 4, 4)] = acc[:, 0]
            ct[it, 1, pl.ds(yy * 4, 4)] = acc[:, 1]
            send(ct.at[it, other, pl.ds(yy * 4, 4)], cp.at[it, pl.ds(yy * 4, 4)], cp_r.at[it, yy], cpart)
        for yy in slabs:
            arrived(cp.at[it, pl.ds(yy * 4, 4)], cp_r.at[it, yy])
            for i in range(4):
                mine, theirs = ct[it, core, yy * 4 + i], cp[it, yy * 4 + i]
                pk[it, yy * 4 + i] = jnp.concatenate(
                    [jnp.where(own_first, mine, theirs), jnp.where(own_first, theirs, mine)], axis=1)
        for c in range(3):
            rows = slice(c * 8, c * 8 + 8)
            for dz in (2, 1, 3, 0):
                for dy in (2, 1, 3, 0):
                    if dy + dz:
                        jj = (y + dy) % 4 * 4 + (zhi + dz) % 4
                        send(pk.at[it, jj, rows], u.at[it, j, rows], u_r.at[it, j, c], dev(dy, dz))
        u[it, j] = pk[it, j]
        square = jnp.concatenate([ct[it, i % 2, i // 2] for i in range(32)], axis=0)
        square = jnp.concatenate([square, jnp.zeros((768, 64), F32)], axis=1).T[:192]
        ch[...] = square + drv[...]

    def mirror(it, c):
        rows = slice(c * 8, c * 8 + 8)
        for dy in (0, 1, 3, 2):
            for dz in (0, 1, 3, 2):
                if dy + dz:
                    jj = (y + dy) % 4 * 4 + (zhi + dz) % 4
                    arrived(u.at[it, jj, rows], u_r.at[it, jj, c])
        for q in range(8):
            xs[it, q, rows] = jnp.concatenate(
                [u[it, i // 2, rows, i % 2 * 192 + q * 24:i % 2 * 192 + q * 24 + 24] for i in range(32)], axis=1)
        for d in (2, 6, 1, 3, 5, 7, 4):
            q = (s + d) % 8
            send(xs.at[it, q, rows], m.at[it, s, rows], m_r.at[it, s, c], (q, t))
        m[it, s, rows] = xs[it, s, rows]

    def update(it, c):
        rows = slice(c * 8, c * 8 + 8)
        for d in range(1, 8):
            q = (s + d) % 8
            arrived(m.at[it, q, rows], m_r.at[it, q, c])
        tot = ch[...].reshape(8, 24, 768)[:, rows] + m[it, :, rows]
        keep = rowi[:, rows] == coli.reshape(1, 1, 768)
        return jnp.where(keep, -tot / (rowe[:, rows] + cole.reshape(1, 1, 768)), 0.0)

    def next_b(c):
        ball[1, c, s] = update(0, c).reshape(64, 768).astype(BF16)
        spread_b(1, c)

    def first_rhs():
        return jnp.concatenate([jnp.concatenate([ball[0, k, q, :, h * 384:h * 384 + 384] for k in range(3)], axis=0)
                                for h in (0, 1) for q in range(8)], axis=1)

    def second_rhs():
        return jnp.concatenate([bn[q, :, h * 384:h * 384 + 384] for h in (0, 1) for q in range(8)], axis=1)

    loads[2].wait()
    cycle(0, first_rhs)
    mirror(0, 0)
    mirror(0, 1)
    next_b(0)
    mirror(0, 2)
    next_b(1)
    onward_b(1, 0, 0)
    partner_b(1, 0)
    next_b(2)
    onward_b(1, 1, 0)
    partner_b(1, 1)
    onward_b(1, 0, 1)
    onward_b(1, 2, 0)
    partner_b(1, 2)
    onward_b(1, 1, 1)
    onward_b(1, 2, 1)
    for k in range(3):
        last_b(1, k)
    for q in range(8):
        thirds = [ball[1, k, q].astype(F32).reshape(8, 8, 768) for k in range(3)]
        bn[q] = jnp.concatenate([thirds[i % 3][i // 3] for i in range(24)], axis=0).astype(BF16)
    cycle(1, second_rhs)
    for c in range(3):
        mirror(1, c)
    for c in range(3):
        out[:, c * 8:c * 8 + 8] = update(1, c)
    for copy in pending:
        copy.wait_send()


def local(amplitudes, driving, cycle_ints, occ_irrep, vir_irrep, occ_energy, vir_energy, slab):
    rows, cols = amplitudes.shape
    rloc = cycle_ints.T.reshape(8, 24, cols)
    dma = pltpu.SemaphoreType.DMA
    vmem = pl.BlockSpec(memory_space=pltpu.VMEM)
    result = pl.pallas_call(
        kernel,
        out_shape=jax.ShapeDtypeStruct((8, 24, cols), F32),
        in_specs=[pl.BlockSpec(memory_space=pl.ANY)] * 3 + [vmem] * 4 + [pl.BlockSpec(memory_space=pltpu.SMEM)],
        out_specs=vmem,
        scratch_shapes=[
            pltpu.VMEM((192, 768), F32),
            pltpu.VMEM((192, 768), F32),
            pltpu.VMEM((8, 24, 768), BF16),
            pltpu.VMEM((8, 24, 768), BF16),
            pltpu.VMEM((8, 48, 384), BF16),
            pltpu.VMEM((16, 48, 6144), BF16),
            pltpu.VMEM((2, 3, 8, 64, 768), BF16),
            pltpu.VMEM((8, 192, 768), BF16),
            pltpu.VMEM((2, 2, 16, 24, 192), F32),
            pltpu.VMEM((2, 16, 24, 192), F32),
            pltpu.VMEM((2, 16, 24, 384), F32),
            pltpu.VMEM((2, 16, 24, 384), F32),
            pltpu.VMEM((2, 8, 24, 768), F32),
            pltpu.VMEM((2, 8, 24, 768), F32),
            pltpu.VMEM((192, 768), F32),
            dma((3,)), dma((512,)), dma, dma((8,)), dma((2, 3, 8, 2)), dma((16, 3)), dma((16, 3)), dma((2, 4)),
            dma((2, 16, 3)), dma((2, 8, 3)),
        ],
        compiler_params=pltpu.CompilerParams(
            collective_id=0, has_side_effects=True, vmem_limit_bytes=48 * 2**20),
        cost_estimate=pl.CostEstimate(flops=2 * 2 * 192 * 768 * 6144, bytes_accessed=3 * 2**20, transcendentals=0),
    )(amplitudes, driving, rloc, vir_energy.reshape(1, -1), vir_irrep.reshape(1, -1),
      occ_energy.reshape(1, -1), occ_irrep.reshape(1, -1), slab)
    return result.reshape(rows, cols)


def solution(mesh):
    in_specs = (P("ta", "ka"), P("ta", "ka"), P("ka", "ta"), P(), P(), P(), P(), P())
    return jax.shard_map(local, mesh=mesh, in_specs=in_specs, out_specs=P("ta", "ka"), check_vma=False)
```

```python
import jax
import jax.numpy as jnp
from jax import lax
from jax.experimental import pallas as pl
from jax.experimental.pallas import tpu as pltpu
from jax.sharding import PartitionSpec as P

MESH = pl.DeviceIdType.MESH
NT = (((1,), (1,)), ((), ()))
F32, BF16 = jnp.float32, jnp.bfloat16


PIECES = ((0, 1408), (1408, 1280), (2688, 384))


def kernel(amp_h, drv_h, rloc_h, vire, viri, occe, occi, slab, out,
           amp, drv, rloc, rpair, rsend, rt, ball, bn, ct, cp, pk, u, xs, m, ch,
           l_s, p_s, p_r, a_s, a_r, g_s, r_r, c_s, c_r, b_s, b0_r, b1_r, cp_s, cp_r, u_s, u_r, m_s, m_r):
    s = lax.axis_index("ka")
    t = lax.axis_index("ta")
    zlo, x = s // 4, s % 4
    y, zhi, core = t // 8, (t // 2) % 4, t % 2
    j = t // 2
    other = 1 - core

    loads = [pltpu.make_async_copy(rloc_h, rloc, l_s.at[0]),
             pltpu.make_async_copy(amp_h, amp, l_s.at[1]),
             pltpu.make_async_copy(drv_h, drv, l_s.at[2])]
    for copy in loads:
        copy.start()

    def dev(dy, dz):
        return (s, ((y + dy) % 4 * 4 + (zhi + dz) % 4) * 2 + core)

    zp = (1 - zlo) * 4 + x
    cpart = (s, j * 2 + other)
    greet = [dev(0, 1), dev(0, 3), dev(1, 0), dev(3, 0)] + [((s + d) % 8, t) for d in (2, 6, 1, 3, 5, 7, 4)] + [cpart]
    barrier = pltpu.get_barrier_semaphore()
    for peer in greet:
        pl.semaphore_signal(barrier, inc=1, device_id=peer, device_id_type=MESH)
    pl.semaphore_wait(barrier, len(greet))

    def send(src, dst, ss, rs, peer):
        pltpu.make_async_remote_copy(
            src_ref=src, dst_ref=dst, send_sem=ss, recv_sem=rs, device_id=peer, device_id_type=MESH).start()

    def arrived(dst, rs):
        pltpu.make_async_remote_copy(
            src_ref=dst, dst_ref=dst, send_sem=p_s, recv_sem=rs, device_id=cpart, device_id_type=MESH).wait_recv()

    def sent(src, ss):
        pltpu.make_async_remote_copy(
            src_ref=src, dst_ref=src, send_sem=ss, recv_sem=p_r, device_id=cpart, device_id_type=MESH).wait_send()

    loads[0].wait()
    send(rloc, rpair, p_s, p_r, cpart)
    loads[1].wait()
    for k in range(3):
        ball[0, k, s] = amp[k * 64:k * 64 + 64].astype(BF16)
    arrived(rpair, p_r)
    own_first = core == 0
    for q in range(8):
        a = rloc[q].astype(F32)
        b = rpair[q].astype(F32)
        both = jnp.concatenate([jnp.where(own_first, a, b), jnp.where(own_first, b, a)], axis=0).astype(BF16)
        rsend[q] = jnp.where(own_first, both[:, :384], both[:, 384:])

    def kslot(q):
        return pl.ds(pl.multiple_of(core * 3072 + q * 384, 384), 384)

    for d in range(1, 8):
        q = (s + d) % 8
        send(rsend.at[q], rt.at[j, :, kslot(s)], a_s, a_r, (q, t))
    rt[j, :, kslot(s)] = rsend[s]

    hot = lax.broadcasted_iota(jnp.int32, (1, 128), 1)

    def slab_at(i):
        here = hot == slab[i]
        return (jnp.sum(jnp.where(here, occe[...], 0.0), axis=1, keepdims=True),
                jnp.sum(jnp.where(here, occi[...], 0), axis=1, keepdims=True))

    def tile_part(v):
        runs = [jnp.concatenate([v[:, i * 192 + q * 24:i * 192 + q * 24 + 24] for i in range(8)], axis=1) for q in range(8)]
        part = runs[0]
        for q in range(1, 8):
            part = jnp.where(s == q, runs[q], part)
        return part

    def row_part(v):
        part = v[:, :192]
        for i in range(1, 8):
            part = jnp.where(t % 8 == i, v[:, i * 192:i * 192 + 192], part)
        return part

    picked = [slab_at(i) for i in range(4)]
    vce, vci = tile_part(vire[...]), tile_part(viri[...])
    cole = jnp.concatenate([vce - picked[i][0] for i in range(4)], axis=1)
    coli = jnp.concatenate([jnp.bitwise_xor(vci, picked[i][1]) for i in range(4)], axis=1)
    rowe_v, rowi_v = slab_at(y)
    rowe_l = row_part(vire[...]) - rowe_v
    rowi_l = jnp.bitwise_xor(row_part(viri[...]), rowi_v).astype(F32)

    def stand(line):
        wide = jnp.concatenate([line, jnp.zeros((1, 64), F32)], axis=1)
        return jnp.broadcast_to(wide, (128, 256)).T[:192, :1]

    rowe = stand(rowe_l).reshape(8, 24, 1)
    rowi = stand(rowi_l).reshape(8, 24, 1)
    coli = coli.astype(F32)

    arrived(rsend.at[0:7], a_r)

    def piece(jj, p, c):
        start, size = PIECES[p]
        return rt.at[jj, :, pl.ds(pl.multiple_of(c * 3072 + start, 128), size)]

    def ahead(jj, p, peer):
        send(piece(jj, p, core), piece(jj, p, core), g_s, r_r.at[jj, p], peer)

    def to_core(jj, p):
        send(piece(jj, p, core), piece(jj, p, core), c_s, c_r, cpart)

    def event(dy, dz, p):
        jj = (y + dy) % 4 * 4 + (zhi + dz) % 4
        arrived(piece(jj, p, core), r_r.at[jj, p])
        if p < 2:
            if dy == 0:
                if (dz, p) == (3, 0):
                    ahead(jj, p, dev(0, 1))
                if (dz, p) == (1, 1):
                    ahead(jj, p, dev(0, 3))
                ahead(jj, p, dev(1, 0))
                ahead(jj, p, dev(3, 0))
            if (dy, p) == (3, 0):
                ahead(jj, p, dev(1, 0))
            if (dy, p) == (1, 1):
                ahead(jj, p, dev(3, 0))
        elif dz == 0:
            for d in (1, 3, 2):
                ahead(jj, p, dev(0, d))
        to_core(jj, p)

    def bpart(k, q, h):
        rows = slice(h * 32, h * 32 + 32)
        return (ball.at[0, :, q, rows], b0_r.at[q, h]) if k is None else (ball.at[1, k, q, rows], b1_r.at[k, q, h])

    def b_to(k, q, h, peer):
        ref, sem = bpart(k, q, h)
        send(ref, ref, b_s.at[0 if k is None else 1], sem, (peer, t))

    def b_at(k, q, h):
        arrived(*bpart(k, q, h))

    def round_x(d):
        return zlo * 4 + (x + d) % 4

    def spread_b(k):
        for h in (0, 1):
            b_to(k, s, h, zp)
        for h in (0, 1):
            b_to(k, s, h, round_x(1))
            b_to(k, s, h, round_x(3))

    def partner_b(k):
        for h in (0, 1):
            b_at(k, zp, h)
            b_to(k, zp, h, round_x(1))
            b_to(k, zp, h, round_x(3))

    def onward_b(k, z, cross=False):
        left = (zlo + z) % 2 * 4 + (x + 3) % 4
        right = (zlo + z) % 2 * 4 + (x + 1) % 4
        for q, h in ((left, 0), (right, 1), (left, 1), (right, 0)):
            b_at(k, q, h)
            if (q is left) == (h == 0):
                b_to(k, q, h, round_x(1) if q is left else round_x(3))
            if cross:
                b_to(k, q, h, zp)

    def last_b(k):
        for z in (0, 1):
            for h in (0, 1):
                b_at(k, (zlo + z) % 2 * 4 + (x + 2) % 4, h)

    def cross_b(k):
        for h in (0, 1):
            b_at(k, round_x(2), h)
            b_to(k, round_x(2), h, zp)

    def crossed_b(k):
        for d in range(4):
            for h in (0, 1):
                b_at(k, (1 - zlo) * 4 + (x + d) % 4, h)

    for p in (0, 1):
        ahead(j, p, dev(0, 1))
        ahead(j, p, dev(0, 3))
        ahead(j, p, dev(1, 0))
        ahead(j, p, dev(3, 0))
    for d in (1, 3):
        ahead(j, 2, dev(d, 0))
    spread_b(None)
    for p in (0, 1, 2):
        to_core(j, p)
    for p in (0, 1):
        for d in (3, 1):
            event(0, d, p)
            event(d, 0, p)
    ahead(j, 2, dev(2, 0))
    for d in (1, 3, 2):
        ahead(j, 2, dev(0, d))
    onward_b(None, 0)
    event(1, 0, 2)
    event(3, 0, 2)
    for p in (0, 1):
        event(0, 2, p)
        event(2, 0, p)
    event(2, 0, 2)
    partner_b(None)
    for p in (0, 1):
        for dz in (3, 1):
            for dy in (3, 1):
                event(dy, dz, p)
    onward_b(None, 1)
    for p in (0, 1):
        for dy in (3, 1):
            event(dy, 2, p)
    for p in (0, 1):
        for dz in (3, 1):
            event(2, dz, p)
    for dz in (1, 3, 2):
        for dy in (0, 1, 3, 2):
            event(dy, dz, 2)
    for p in (0, 1):
        event(2, 2, p)
    last_b(None)
    arrived(rt.at[:, :, pl.ds(pl.multiple_of(other * 3072, 3072), 3072)], c_r)

    def cycle(it, rhs):
        steps = (2, 1, 3, 0)
        slabs = [(y + d) % 4 for d in steps]

        def product(yy):
            left = rt[pl.ds(yy * 4, 4)].reshape(192, 6144)
            acc = lax.dot_general(left, rhs(), NT, preferred_element_type=F32).reshape(4, 2, 24, 192)
            ct[it, 0, pl.ds(yy * 4, 4)] = acc[:, 0]
            ct[it, 1, pl.ds(yy * 4, 4)] = acc[:, 1]
            send(ct.at[it, other, pl.ds(yy * 4, 4)], cp.at[it, pl.ds(yy * 4, 4)], cp_s.at[it], cp_r.at[it, yy], cpart)

        def to_mirror(dy, c):
            rows = slice(c * 8, c * 8 + 8)
            for dz in (2, 1, 3, 0):
                if dy + dz:
                    jj = (y + dy) % 4 * 4 + (zhi + dz) % 4
                    send(pk.at[it, jj, rows], u.at[it, j, rows], u_s.at[it], u_r.at[it, c], dev(dy, dz))

        def pack(g):
            yy = slabs[g]
            arrived(cp.at[it, pl.ds(yy * 4, 4)], cp_r.at[it, yy])
            for i in range(4):
                mine, theirs = ct[it, core, yy * 4 + i], cp[it, yy * 4 + i]
                pk[it, yy * 4 + i] = jnp.concatenate(
                    [jnp.where(own_first, mine, theirs), jnp.where(own_first, theirs, mine)], axis=1)
            to_mirror(steps[g], 0)

        product(slabs[0])
        for g in range(1, 4):
            product(slabs[g])
            pack(g - 1)
        pack(3)
        for c in (1, 2):
            for dy in steps:
                to_mirror(dy, c)
        u[it, j] = pk[it, j]
        square = jnp.concatenate([ct[it, i % 2, i // 2] for i in range(32)], axis=0)
        square = jnp.concatenate([square, jnp.zeros((768, 64), F32)], axis=1).T[:192]
        ch[...] = square + drv[...]

    def mirror(it, c):
        rows = slice(c * 8, c * 8 + 8)
        arrived(u.at[it, 0:15, rows], u_r.at[it, c])
        for q in range(8):
            xs[it, q, rows] = jnp.concatenate(
                [u[it, i // 2, rows, i % 2 * 192 + q * 24:i % 2 * 192 + q * 24 + 24] for i in range(32)], axis=1)
        for d in (2, 6, 1, 3, 5, 7, 4):
            q = (s + d) % 8
            send(xs.at[it, q, rows], m.at[it, s, rows], m_s.at[it], m_r.at[it, c], (q, t))
        m[it, s, rows] = xs[it, s, rows]

    def update(it, c):
        rows = slice(c * 8, c * 8 + 8)
        arrived(m.at[it, 0:7, rows], m_r.at[it, c])
        tot = ch[...].reshape(8, 24, 768)[:, rows] + m[it, :, rows]
        keep = rowi[:, rows] == coli.reshape(1, 1, 768)
        return jnp.where(keep, -tot / (rowe[:, rows] + cole.reshape(1, 1, 768)), 0.0)

    def next_b(c):
        ball[1, c, s] = update(0, c).reshape(64, 768).astype(BF16)
        spread_b(c)

    def first_rhs():
        return jnp.concatenate([jnp.concatenate([ball[0, k, q, :, h * 384:h * 384 + 384] for k in range(3)], axis=0)
                                for h in (0, 1) for q in range(8)], axis=1)

    def second_rhs():
        return jnp.concatenate([bn[q, :, h * 384:h * 384 + 384] for h in (0, 1) for q in range(8)], axis=1)

    loads[2].wait()
    cycle(0, first_rhs)
    mirror(0, 0)
    mirror(0, 1)
    next_b(0)
    mirror(0, 2)
    next_b(1)
    onward_b(0, 0)
    partner_b(0)
    next_b(2)
    onward_b(1, 0, cross=True)
    cross_b(1)
    onward_b(0, 1)
    onward_b(2, 0)
    partner_b(2)
    onward_b(2, 1)
    last_b(0)
    crossed_b(1)
    last_b(2)
    for q in range(8):
        thirds = [ball[1, k, q].astype(F32).reshape(8, 8, 768) for k in range(3)]
        bn[q] = jnp.concatenate([thirds[i % 3][i // 3] for i in range(24)], axis=0).astype(BF16)
    cycle(1, second_rhs)
    for c in range(3):
        mirror(1, c)
    for c in range(3):
        out[:, c * 8:c * 8 + 8] = update(1, c)
    sent(rloc, p_s)
    sent(rsend.at[0:7], a_s)
    sent(rt.at[0:15, :, 0:3072], g_s)
    sent(rt.at[:, :, 0:3072], c_s)
    for it in (0, 1):
        sent(ball.at[it, :, 0:7], b_s.at[it])
        sent(cp.at[it], cp_s.at[it])
        sent(pk.at[it, 0:15], u_s.at[it])
        sent(xs.at[it, 0:7], m_s.at[it])


def local(amplitudes, driving, cycle_ints, occ_irrep, vir_irrep, occ_energy, vir_energy, slab):
    rows, cols = amplitudes.shape
    rloc = cycle_ints.T.reshape(8, 24, cols)
    dma = pltpu.SemaphoreType.DMA
    vmem = pl.BlockSpec(memory_space=pltpu.VMEM)
    result = pl.pallas_call(
        kernel,
        out_shape=jax.ShapeDtypeStruct((8, 24, cols), F32),
        in_specs=[pl.BlockSpec(memory_space=pltpu.HBM)] * 3 + [vmem] * 4 + [pl.BlockSpec(memory_space=pltpu.SMEM)],
        out_specs=vmem,
        scratch_shapes=[
            pltpu.VMEM((192, 768), F32),
            pltpu.VMEM((192, 768), F32),
            pltpu.VMEM((8, 24, 768), BF16),
            pltpu.VMEM((8, 24, 768), BF16),
            pltpu.VMEM((8, 48, 384), BF16),
            pltpu.VMEM((16, 48, 6144), BF16),
            pltpu.VMEM((2, 3, 8, 64, 768), BF16),
            pltpu.VMEM((8, 192, 768), BF16),
            pltpu.VMEM((2, 2, 16, 24, 192), F32),
            pltpu.VMEM((2, 16, 24, 192), F32),
            pltpu.VMEM((2, 16, 24, 384), F32),
            pltpu.VMEM((2, 16, 24, 384), F32),
            pltpu.VMEM((2, 8, 24, 768), F32),
            pltpu.VMEM((2, 8, 24, 768), F32),
            pltpu.VMEM((192, 768), F32),
            dma((3,)), dma, dma, dma, dma, dma, dma((16, 3)), dma, dma, dma((2,)), dma((8, 2)), dma((3, 8, 2)),
            dma((2,)), dma((2, 4)), dma((2,)), dma((2, 3)), dma((2,)), dma((2, 3)),
        ],
        compiler_params=pltpu.CompilerParams(
            collective_id=0, has_side_effects=True, vmem_limit_bytes=48 * 2**20),
        cost_estimate=pl.CostEstimate(flops=2 * 2 * 192 * 768 * 6144, bytes_accessed=3 * 2**20, transcendentals=0),
    )(amplitudes, driving, rloc, vir_energy.reshape(1, -1), vir_irrep.reshape(1, -1),
      occ_energy.reshape(1, -1), occ_irrep.reshape(1, -1), slab)
    return result.reshape(rows, cols)


def solution(mesh):
    in_specs = (P("ta", "ka"), P("ta", "ka"), P("ka", "ta"), P(), P(), P(), P(), P())
    return jax.shard_map(local, mesh=mesh, in_specs=in_specs, out_specs=P("ta", "ka"), check_vma=False)
```

```python
import jax
import jax.numpy as jnp
from jax import lax
from jax.experimental import pallas as pl
from jax.experimental.pallas import tpu as pltpu
from jax.sharding import PartitionSpec as P

MESH = pl.DeviceIdType.MESH
NT = (((1,), (1,)), ((), ()))
F32, BF16 = jnp.float32, jnp.bfloat16


PIECES = ((0, 1408), (1408, 1280), (2688, 384))


def kernel(amp_h, drv_h, rloc_h, vire, viri, occe, occi, slab, out,
           amp, drv, rloc, rpair, rsend, rt, ball, bn, ct, cp, pk, u, xs, m, ch,
           l_s, p_s, p_r, a_s, a_r, g_s, r_r, c_s, c_r, b_s, b0_r, b1_r, cp_s, cp_r, u_s, u_r, m_s, m_r):
    s = lax.axis_index("ka")
    t = lax.axis_index("ta")
    zlo, x = s // 4, s % 4
    y, zhi, core = t // 8, (t // 2) % 4, t % 2
    j = t // 2
    other = 1 - core

    loads = [pltpu.make_async_copy(rloc_h, rloc, l_s.at[0]),
             pltpu.make_async_copy(amp_h, amp, l_s.at[1]),
             pltpu.make_async_copy(drv_h, drv, l_s.at[2])]
    for copy in loads:
        copy.start()

    def dev(dy, dz):
        return (s, ((y + dy) % 4 * 4 + (zhi + dz) % 4) * 2 + core)

    zp = (1 - zlo) * 4 + x
    cpart = (s, j * 2 + other)
    greet = [dev(0, 1), dev(0, 3), dev(1, 0), dev(3, 0)] + [((s + d) % 8, t) for d in (2, 6, 1, 3, 5, 7, 4)] + [cpart]
    barrier = pltpu.get_barrier_semaphore()
    for peer in greet:
        pl.semaphore_signal(barrier, inc=1, device_id=peer, device_id_type=MESH)
    pl.semaphore_wait(barrier, len(greet))

    def send(src, dst, ss, rs, peer):
        pltpu.make_async_remote_copy(
            src_ref=src, dst_ref=dst, send_sem=ss, recv_sem=rs, device_id=peer, device_id_type=MESH).start()

    def arrived(dst, rs):
        pltpu.make_async_remote_copy(
            src_ref=dst, dst_ref=dst, send_sem=p_s, recv_sem=rs, device_id=cpart, device_id_type=MESH).wait_recv()

    def sent(src, ss):
        pltpu.make_async_remote_copy(
            src_ref=src, dst_ref=src, send_sem=ss, recv_sem=p_r, device_id=cpart, device_id_type=MESH).wait_send()

    loads[0].wait()
    send(rloc, rpair, p_s, p_r, cpart)
    loads[1].wait()
    for k in range(3):
        ball[0, k, s] = amp[k * 64:k * 64 + 64].astype(BF16)
    arrived(rpair, p_r)
    own_first = core == 0
    for q in range(8):
        a = rloc[q].astype(F32)
        b = rpair[q].astype(F32)
        both = jnp.concatenate([jnp.where(own_first, a, b), jnp.where(own_first, b, a)], axis=0).astype(BF16)
        rsend[q] = jnp.where(own_first, both[:, :384], both[:, 384:])

    def kslot(q):
        return pl.ds(pl.multiple_of(core * 3072 + q * 384, 384), 384)

    for d in range(1, 8):
        q = (s + d) % 8
        send(rsend.at[q], rt.at[j, :, kslot(s)], a_s, a_r, (q, t))
    rt[j, :, kslot(s)] = rsend[s]

    hot = lax.broadcasted_iota(jnp.int32, (1, 128), 1)

    def slab_at(i):
        here = hot == slab[i]
        return (jnp.sum(jnp.where(here, occe[...], 0.0), axis=1, keepdims=True),
                jnp.sum(jnp.where(here, occi[...], 0), axis=1, keepdims=True))

    def tile_part(v):
        runs = [jnp.concatenate([v[:, i * 192 + q * 24:i * 192 + q * 24 + 24] for i in range(8)], axis=1) for q in range(8)]
        part = runs[0]
        for q in range(1, 8):
            part = jnp.where(s == q, runs[q], part)
        return part

    def row_part(v):
        part = v[:, :192]
        for i in range(1, 8):
            part = jnp.where(t % 8 == i, v[:, i * 192:i * 192 + 192], part)
        return part

    picked = [slab_at(i) for i in range(4)]
    vce, vci = tile_part(vire[...]), tile_part(viri[...])
    cole = jnp.concatenate([vce - picked[i][0] for i in range(4)], axis=1)
    coli = jnp.concatenate([jnp.bitwise_xor(vci, picked[i][1]) for i in range(4)], axis=1)
    rowe_v, rowi_v = slab_at(y)
    rowe_l = row_part(vire[...]) - rowe_v
    rowi_l = jnp.bitwise_xor(row_part(viri[...]), rowi_v).astype(F32)

    def stand(line):
        wide = jnp.concatenate([line, jnp.zeros((1, 64), F32)], axis=1)
        return jnp.broadcast_to(wide, (128, 256)).T[:192, :1]

    rowe = stand(rowe_l).reshape(8, 24, 1)
    rowi = stand(rowi_l).reshape(8, 24, 1)
    coli = coli.astype(F32)

    arrived(rsend.at[0:7], a_r)

    def piece(jj, p, c):
        start, size = PIECES[p]
        return rt.at[jj, :, pl.ds(pl.multiple_of(c * 3072 + start, 128), size)]

    def ahead(jj, p, peer):
        send(piece(jj, p, core), piece(jj, p, core), g_s, r_r.at[jj, p], peer)

    def to_core(jj, p):
        send(piece(jj, p, core), piece(jj, p, core), c_s, c_r.at[jj // 4], cpart)

    def event(dy, dz, p):
        jj = (y + dy) % 4 * 4 + (zhi + dz) % 4
        arrived(piece(jj, p, core), r_r.at[jj, p])
        if p < 2:
            if dy == 0:
                if (dz, p) == (3, 0):
                    ahead(jj, p, dev(0, 1))
                if (dz, p) == (1, 1):
                    ahead(jj, p, dev(0, 3))
                ahead(jj, p, dev(1, 0))
                ahead(jj, p, dev(3, 0))
            if (dy, p) == (3, 0):
                ahead(jj, p, dev(1, 0))
            if (dy, p) == (1, 1):
                ahead(jj, p, dev(3, 0))
        elif dz == 0:
            for d in (1, 3, 2):
                ahead(jj, p, dev(0, d))
        to_core(jj, p)

    def bpart(k, q, h):
        rows = slice(h * 32, h * 32 + 32)
        return (ball.at[0, :, q, rows], b0_r.at[q, h]) if k is None else (ball.at[1, k, q, rows], b1_r.at[k, q, h])

    def b_to(k, q, h, peer):
        ref, sem = bpart(k, q, h)
        send(ref, ref, b_s.at[0 if k is None else 1], sem, (peer, t))

    def b_at(k, q, h):
        arrived(*bpart(k, q, h))

    def round_x(d):
        return zlo * 4 + (x + d) % 4

    def spread_b(k):
        for h in (0, 1):
            b_to(k, s, h, zp)
        for h in (0, 1):
            b_to(k, s, h, round_x(1))
            b_to(k, s, h, round_x(3))

    def partner_b(k):
        for h in (0, 1):
            b_at(k, zp, h)
            b_to(k, zp, h, round_x(1))
            b_to(k, zp, h, round_x(3))

    def onward_b(k, z, cross=False):
        left = (zlo + z) % 2 * 4 + (x + 3) % 4
        right = (zlo + z) % 2 * 4 + (x + 1) % 4
        for q, h in ((left, 0), (right, 1), (left, 1), (right, 0)):
            b_at(k, q, h)
            if (q is left) == (h == 0):
                b_to(k, q, h, round_x(1) if q is left else round_x(3))
            if cross:
                b_to(k, q, h, zp)

    def last_b(k):
        for z in (0, 1):
            for h in (0, 1):
                b_at(k, (zlo + z) % 2 * 4 + (x + 2) % 4, h)

    def cross_b(k):
        for h in (0, 1):
            b_at(k, round_x(2), h)
            b_to(k, round_x(2), h, zp)

    def crossed_b(k):
        for d in range(4):
            for h in (0, 1):
                b_at(k, (1 - zlo) * 4 + (x + d) % 4, h)

    def product(it, dy, rhs):
        yy = (y + dy) % 4
        left = rt[pl.ds(yy * 4, 4)].reshape(192, 6144)
        acc = lax.dot_general(left, rhs(), NT, preferred_element_type=F32).reshape(4, 2, 24, 192)
        ct[it, 0, pl.ds(yy * 4, 4)] = acc[:, 0]
        ct[it, 1, pl.ds(yy * 4, 4)] = acc[:, 1]
        send(ct.at[it, other, pl.ds(yy * 4, 4)], cp.at[it, pl.ds(yy * 4, 4)], cp_s.at[it], cp_r.at[it, yy], cpart)

    def pack(it, dy):
        yy = (y + dy) % 4
        arrived(cp.at[it, pl.ds(yy * 4, 4)], cp_r.at[it, yy])
        for i in range(4):
            mine, theirs = ct[it, core, yy * 4 + i], cp[it, yy * 4 + i]
            pk[it, yy * 4 + i] = jnp.concatenate(
                [jnp.where(own_first, mine, theirs), jnp.where(own_first, theirs, mine)], axis=1)

    def to_mirror(it, dy, c):
        rows = slice(c * 8, c * 8 + 8)
        for dz in (2, 1, 3, 0):
            if dy + dz:
                jj = (y + dy) % 4 * 4 + (zhi + dz) % 4
                send(pk.at[it, jj, rows], u.at[it, j, rows], u_s.at[it], u_r.at[it, c], dev(dy, dz))

    def square(it):
        u[it, j] = pk[it, j]
        c = jnp.concatenate([ct[it, i % 2, i // 2] for i in range(32)], axis=0)
        ch[...] = jnp.concatenate([c, jnp.zeros((768, 64), F32)], axis=1).T[:192] + drv[...]

    def first_rhs():
        return jnp.concatenate([jnp.concatenate([ball[0, k, q, :, h * 384:h * 384 + 384] for k in range(3)], axis=0)
                                for h in (0, 1) for q in range(8)], axis=1)

    def second_rhs():
        return jnp.concatenate([bn[q, :, h * 384:h * 384 + 384] for h in (0, 1) for q in range(8)], axis=1)

    def first_group(dy):
        yy = (y + dy) % 4
        arrived(rt.at[pl.ds(yy * 4, 4), :, pl.ds(pl.multiple_of(other * 3072, 3072), 3072)], c_r.at[yy])
        product(0, dy, first_rhs)
        pack(0, dy)
        for c in range(3):
            to_mirror(0, dy, c)

    for p in (0, 1):
        ahead(j, p, dev(0, 1))
        ahead(j, p, dev(0, 3))
        ahead(j, p, dev(1, 0))
        ahead(j, p, dev(3, 0))
    for d in (1, 3):
        ahead(j, 2, dev(d, 0))
    for p in (0, 1, 2):
        to_core(j, p)
    for p in (0, 1):
        for d in (3, 1):
            event(0, d, p)
            event(d, 0, p)
    spread_b(None)
    ahead(j, 2, dev(2, 0))
    event(1, 0, 2)
    event(3, 0, 2)
    for p in (0, 1):
        event(0, 2, p)
        event(2, 0, p)
    event(2, 0, 2)
    for d in (1, 3, 2):
        ahead(j, 2, dev(0, d))
    onward_b(None, 0)
    for dz in (3, 1):
        for dy in (3, 1):
            event(dy, dz, 0)
    partner_b(None)
    for dz in (3, 1):
        for dy in (3, 1):
            event(dy, dz, 1)
    for p in (0, 1):
        for dy in (3, 1):
            event(dy, 2, p)
    onward_b(None, 1)
    for dz in (1, 3, 2):
        event(0, dz, 2)
    last_b(None)
    loads[2].wait()
    for dy in (1, 3):
        for dz in (1, 3, 2):
            event(dy, dz, 2)
    for p in (0, 1):
        for dz in (3, 1):
            event(2, dz, p)
    for p in (0, 1):
        event(2, 2, p)
    for dz in (1, 3, 2):
        event(2, dz, 2)
    for dy in (2, 1, 3, 0):
        first_group(dy)
    square(0)

    def mirror(it, c):
        rows = slice(c * 8, c * 8 + 8)
        arrived(u.at[it, 0:15, rows], u_r.at[it, c])
        for q in range(8):
            xs[it, q, rows] = jnp.concatenate(
                [u[it, i // 2, rows, i % 2 * 192 + q * 24:i % 2 * 192 + q * 24 + 24] for i in range(32)], axis=1)
        for d in (2, 6, 1, 3, 5, 7, 4):
            q = (s + d) % 8
            send(xs.at[it, q, rows], m.at[it, s, rows], m_s.at[it], m_r.at[it, c], (q, t))
        m[it, s, rows] = xs[it, s, rows]

    def update(it, c):
        rows = slice(c * 8, c * 8 + 8)
        arrived(m.at[it, 0:7, rows], m_r.at[it, c])
        tot = ch[...].reshape(8, 24, 768)[:, rows] + m[it, :, rows]
        keep = rowi[:, rows] == coli.reshape(1, 1, 768)
        return jnp.where(keep, -tot / (rowe[:, rows] + cole.reshape(1, 1, 768)), 0.0)

    def next_b(c):
        ball[1, c, s] = update(0, c).reshape(64, 768).astype(BF16)
        spread_b(c)

    mirror(0, 0)
    mirror(0, 1)
    next_b(0)
    mirror(0, 2)
    next_b(1)
    onward_b(0, 0)
    partner_b(0)
    next_b(2)
    onward_b(1, 0, cross=True)
    cross_b(1)
    onward_b(0, 1)
    onward_b(2, 0)
    partner_b(2)
    onward_b(2, 1)
    last_b(0)
    crossed_b(1)
    last_b(2)
    for q in range(8):
        thirds = [ball[1, k, q].astype(F32).reshape(8, 8, 768) for k in range(3)]
        bn[q] = jnp.concatenate([thirds[i % 3][i // 3] for i in range(24)], axis=0).astype(BF16)
    steps = (2, 1, 3, 0)
    product(1, steps[0], second_rhs)
    for g in range(1, 4):
        product(1, steps[g], second_rhs)
        pack(1, steps[g - 1])
        to_mirror(1, steps[g - 1], 0)
    pack(1, steps[3])
    to_mirror(1, steps[3], 0)
    for c in (1, 2):
        for dy in steps:
            to_mirror(1, dy, c)
    square(1)
    for c in range(3):
        mirror(1, c)
    for c in range(3):
        out[:, c * 8:c * 8 + 8] = update(1, c)
    sent(rloc, p_s)
    sent(rsend.at[0:7], a_s)
    sent(rt.at[0:15, :, 0:3072], g_s)
    sent(rt.at[:, :, 0:3072], c_s)
    for it in (0, 1):
        sent(ball.at[it, :, 0:7], b_s.at[it])
        sent(cp.at[it], cp_s.at[it])
        sent(pk.at[it, 0:15], u_s.at[it])
        sent(xs.at[it, 0:7], m_s.at[it])


def local(amplitudes, driving, cycle_ints, occ_irrep, vir_irrep, occ_energy, vir_energy, slab):
    rows, cols = amplitudes.shape
    rloc = cycle_ints.T.reshape(8, 24, cols)
    dma = pltpu.SemaphoreType.DMA
    vmem = pl.BlockSpec(memory_space=pltpu.VMEM)
    result = pl.pallas_call(
        kernel,
        out_shape=jax.ShapeDtypeStruct((8, 24, cols), F32),
        in_specs=[pl.BlockSpec(memory_space=pltpu.HBM)] * 3 + [vmem] * 4 + [pl.BlockSpec(memory_space=pltpu.SMEM)],
        out_specs=vmem,
        scratch_shapes=[
            pltpu.VMEM((192, 768), F32),
            pltpu.VMEM((192, 768), F32),
            pltpu.VMEM((8, 24, 768), BF16),
            pltpu.VMEM((8, 24, 768), BF16),
            pltpu.VMEM((8, 48, 384), BF16),
            pltpu.VMEM((16, 48, 6144), BF16),
            pltpu.VMEM((2, 3, 8, 64, 768), BF16),
            pltpu.VMEM((8, 192, 768), BF16),
            pltpu.VMEM((2, 2, 16, 24, 192), F32),
            pltpu.VMEM((2, 16, 24, 192), F32),
            pltpu.VMEM((2, 16, 24, 384), F32),
            pltpu.VMEM((2, 16, 24, 384), F32),
            pltpu.VMEM((2, 8, 24, 768), F32),
            pltpu.VMEM((2, 8, 24, 768), F32),
            pltpu.VMEM((192, 768), F32),
            dma((3,)), dma, dma, dma, dma, dma, dma((16, 3)), dma, dma((4,)), dma((2,)), dma((8, 2)), dma((3, 8, 2)),
            dma((2,)), dma((2, 4)), dma((2,)), dma((2, 3)), dma((2,)), dma((2, 3)),
        ],
        compiler_params=pltpu.CompilerParams(
            collective_id=0, has_side_effects=True, vmem_limit_bytes=63 * 2**20),
        cost_estimate=pl.CostEstimate(flops=2 * 2 * 192 * 768 * 6144, bytes_accessed=3 * 2**20, transcendentals=0),
    )(amplitudes, driving, rloc, vir_energy.reshape(1, -1), vir_irrep.reshape(1, -1),
      occ_energy.reshape(1, -1), occ_irrep.reshape(1, -1), slab)
    return result.reshape(rows, cols)


def solution(mesh):
    in_specs = (P("ta", "ka"), P("ta", "ka"), P("ka", "ta"), P(), P(), P(), P(), P())
    return jax.shard_map(local, mesh=mesh, in_specs=in_specs, out_specs=P("ta", "ka"), check_vma=False)
```

```python
import jax
import jax.numpy as jnp
from jax import lax
from jax.experimental import pallas as pl
from jax.experimental.pallas import tpu as pltpu
from jax.sharding import PartitionSpec as P

MESH = pl.DeviceIdType.MESH
NT = (((1,), (1,)), ((), ()))
F32, BF16 = jnp.float32, jnp.bfloat16


PIECES = ((0, 1408), (1408, 1280), (2688, 384))


def kernel(amp_h, drv_h, rloc_h, vire, viri, occe, occi, slab, out,
           amp, drv, rloc, rpair, rsend, rt, ball, bn, ct, cp, pk, u, xs, m, ch,
           l_s, p_s, p_r, a_s, a_r, g_s, r_r, c_s, c_r, b_s, b0_r, b1_r, cp_s, cp_r, u_s, u_r, m_s, m_r):
    s = lax.axis_index("ka")
    t = lax.axis_index("ta")
    zlo, x = s // 4, s % 4
    y, zhi, core = t // 8, (t // 2) % 4, t % 2
    j = t // 2
    other = 1 - core

    loads = [pltpu.make_async_copy(rloc_h, rloc, l_s.at[0]),
             pltpu.make_async_copy(amp_h, amp, l_s.at[1]),
             pltpu.make_async_copy(drv_h, drv, l_s.at[2])]
    for copy in loads:
        copy.start()

    def dev(dy, dz):
        return (s, ((y + dy) % 4 * 4 + (zhi + dz) % 4) * 2 + core)

    zp = (1 - zlo) * 4 + x
    cpart = (s, j * 2 + other)
    greet = [dev(0, 1), dev(0, 3), dev(1, 0), dev(3, 0)] + [((s + d) % 8, t) for d in (2, 6, 1, 3, 5, 7, 4)] + [cpart]
    barrier = pltpu.get_barrier_semaphore()
    for peer in greet:
        pl.semaphore_signal(barrier, inc=1, device_id=peer, device_id_type=MESH)
    pl.semaphore_wait(barrier, len(greet))

    def send(src, dst, ss, rs, peer):
        pltpu.make_async_remote_copy(
            src_ref=src, dst_ref=dst, send_sem=ss, recv_sem=rs, device_id=peer, device_id_type=MESH).start()

    def arrived(dst, rs):
        pltpu.make_async_remote_copy(
            src_ref=dst, dst_ref=dst, send_sem=p_s, recv_sem=rs, device_id=cpart, device_id_type=MESH).wait_recv()

    def sent(src, ss):
        pltpu.make_async_remote_copy(
            src_ref=src, dst_ref=src, send_sem=ss, recv_sem=p_r, device_id=cpart, device_id_type=MESH).wait_send()

    loads[0].wait()
    send(rloc, rpair, p_s, p_r, cpart)
    loads[1].wait()
    for k in range(3):
        ball[0, k, s] = amp[k * 64:k * 64 + 64].astype(BF16)
    arrived(rpair, p_r)
    own_first = core == 0
    for q in range(8):
        a = rloc[q].astype(F32)
        b = rpair[q].astype(F32)
        both = jnp.concatenate([jnp.where(own_first, a, b), jnp.where(own_first, b, a)], axis=0).astype(BF16)
        rsend[q] = jnp.where(own_first, both[:, :384], both[:, 384:])

    def kslot(q):
        return pl.ds(pl.multiple_of(core * 3072 + q * 384, 384), 384)

    for d in range(1, 8):
        q = (s + d) % 8
        send(rsend.at[q], rt.at[j, :, kslot(s)], a_s, a_r, (q, t))
    rt[j, :, kslot(s)] = rsend[s]

    hot = lax.broadcasted_iota(jnp.int32, (1, 128), 1)

    def slab_at(i):
        here = hot == slab[i]
        return (jnp.sum(jnp.where(here, occe[...], 0.0), axis=1, keepdims=True),
                jnp.sum(jnp.where(here, occi[...], 0), axis=1, keepdims=True))

    def tile_part(v):
        runs = [jnp.concatenate([v[:, i * 192 + q * 24:i * 192 + q * 24 + 24] for i in range(8)], axis=1) for q in range(8)]
        part = runs[0]
        for q in range(1, 8):
            part = jnp.where(s == q, runs[q], part)
        return part

    def row_part(v):
        part = v[:, :192]
        for i in range(1, 8):
            part = jnp.where(t % 8 == i, v[:, i * 192:i * 192 + 192], part)
        return part

    picked = [slab_at(i) for i in range(4)]
    vir_e = jnp.concatenate([vire[i:i + 1] for i in range(12)], axis=1)
    vir_i = jnp.concatenate([viri[i:i + 1] for i in range(12)], axis=1)
    vce, vci = tile_part(vir_e), tile_part(vir_i)
    cole = jnp.concatenate([vce - picked[i][0] for i in range(4)], axis=1)
    coli = jnp.concatenate([jnp.bitwise_xor(vci, picked[i][1]) for i in range(4)], axis=1)
    rowe_v, rowi_v = slab_at(y)
    rowe_l = row_part(vir_e) - rowe_v
    rowi_l = jnp.bitwise_xor(row_part(vir_i), rowi_v).astype(F32)

    def stand(line):
        wide = jnp.concatenate([line, jnp.zeros((1, 64), F32)], axis=1)
        return jnp.broadcast_to(wide, (128, 256)).T[:192, :1]

    rowe = stand(rowe_l).reshape(8, 24, 1)
    rowi = stand(rowi_l).reshape(8, 24, 1)
    coli = coli.astype(F32)

    arrived(rsend.at[0:7], a_r)

    def piece(jj, p, c):
        start, size = PIECES[p]
        return rt.at[jj, :, pl.ds(pl.multiple_of(c * 3072 + start, 128), size)]

    def ahead(jj, p, peer):
        send(piece(jj, p, core), piece(jj, p, core), g_s, r_r.at[jj, p], peer)

    def to_core(jj, p):
        send(piece(jj, p, core), piece(jj, p, core), c_s, c_r.at[jj // 4], cpart)

    def event(dy, dz, p):
        jj = (y + dy) % 4 * 4 + (zhi + dz) % 4
        arrived(piece(jj, p, core), r_r.at[jj, p])
        if p < 2:
            if dy == 0:
                if (dz, p) == (3, 0):
                    ahead(jj, p, dev(0, 1))
                if (dz, p) == (1, 1):
                    ahead(jj, p, dev(0, 3))
                ahead(jj, p, dev(1, 0))
                ahead(jj, p, dev(3, 0))
            if (dy, p) == (3, 0):
                ahead(jj, p, dev(1, 0))
            if (dy, p) == (1, 1):
                ahead(jj, p, dev(3, 0))
        elif dz == 0:
            for d in (1, 3, 2):
                ahead(jj, p, dev(0, d))
        to_core(jj, p)

    def bpart(k, q, h):
        rows = slice(h * 32, h * 32 + 32)
        return (ball.at[0, :, q, rows], b0_r.at[q, h]) if k is None else (ball.at[1, k, q, rows], b1_r.at[k, q, h])

    def b_to(k, q, h, peer):
        ref, sem = bpart(k, q, h)
        send(ref, ref, b_s.at[0 if k is None else 1], sem, (peer, t))

    def b_at(k, q, h):
        arrived(*bpart(k, q, h))

    def round_x(d):
        return zlo * 4 + (x + d) % 4

    def spread_b(k):
        for h in (0, 1):
            b_to(k, s, h, zp)
        for h in (0, 1):
            b_to(k, s, h, round_x(1))
            b_to(k, s, h, round_x(3))

    def partner_b(k):
        for h in (0, 1):
            b_at(k, zp, h)
            b_to(k, zp, h, round_x(1))
            b_to(k, zp, h, round_x(3))

    def onward_b(k, z, cross=False):
        left = (zlo + z) % 2 * 4 + (x + 3) % 4
        right = (zlo + z) % 2 * 4 + (x + 1) % 4
        for q, h in ((left, 0), (right, 1), (left, 1), (right, 0)):
            b_at(k, q, h)
            if (q is left) == (h == 0):
                b_to(k, q, h, round_x(1) if q is left else round_x(3))
            if cross:
                b_to(k, q, h, zp)

    def last_b(k):
        for z in (0, 1):
            for h in (0, 1):
                b_at(k, (zlo + z) % 2 * 4 + (x + 2) % 4, h)

    def cross_b(k):
        for h in (0, 1):
            b_at(k, round_x(2), h)
            b_to(k, round_x(2), h, zp)

    def crossed_b(k):
        for d in range(4):
            for h in (0, 1):
                b_at(k, (1 - zlo) * 4 + (x + d) % 4, h)

    def product(it, dy, rhs):
        yy = (y + dy) % 4
        left = rt[pl.ds(yy * 4, 4)].reshape(192, 6144)
        acc = lax.dot_general(left, rhs(), NT, preferred_element_type=F32).reshape(4, 2, 24, 192)
        ct[it, 0, pl.ds(yy * 4, 4)] = acc[:, 0]
        ct[it, 1, pl.ds(yy * 4, 4)] = acc[:, 1]
        send(ct.at[it, other, pl.ds(yy * 4, 4)], cp.at[it, pl.ds(yy * 4, 4)], cp_s.at[it], cp_r.at[it, yy], cpart)

    def pack(it, dy):
        yy = (y + dy) % 4
        arrived(cp.at[it, pl.ds(yy * 4, 4)], cp_r.at[it, yy])
        for i in range(4):
            mine, theirs = ct[it, core, yy * 4 + i], cp[it, yy * 4 + i]
            pk[it, yy * 4 + i] = jnp.concatenate(
                [jnp.where(own_first, mine, theirs), jnp.where(own_first, theirs, mine)], axis=1)

    def to_mirror(it, dy, c):
        rows = slice(c * 8, c * 8 + 8)
        for dz in (2, 1, 3, 0):
            if dy + dz:
                jj = (y + dy) % 4 * 4 + (zhi + dz) % 4
                send(pk.at[it, jj, rows], u.at[it, j, rows], u_s.at[it], u_r.at[it, c], dev(dy, dz))

    def square(it):
        u[it, j] = pk[it, j]
        c = jnp.concatenate([ct[it, i % 2, i // 2] for i in range(32)], axis=0)
        ch[...] = jnp.concatenate([c, jnp.zeros((768, 64), F32)], axis=1).T[:192] + drv[...]

    def first_rhs():
        return jnp.concatenate([jnp.concatenate([ball[0, k, q, :, h * 384:h * 384 + 384] for k in range(3)], axis=0)
                                for h in (0, 1) for q in range(8)], axis=1)

    def second_rhs():
        return jnp.concatenate([bn[q, :, h * 384:h * 384 + 384] for h in (0, 1) for q in range(8)], axis=1)

    def first_group(dy):
        yy = (y + dy) % 4
        arrived(rt.at[pl.ds(yy * 4, 4), :, pl.ds(pl.multiple_of(other * 3072, 3072), 3072)], c_r.at[yy])
        product(0, dy, first_rhs)
        pack(0, dy)
        for c in range(3):
            to_mirror(0, dy, c)

    for p in (0, 1):
        ahead(j, p, dev(0, 1))
        ahead(j, p, dev(0, 3))
        ahead(j, p, dev(1, 0))
        ahead(j, p, dev(3, 0))
    for d in (1, 3):
        ahead(j, 2, dev(d, 0))
    for p in (0, 1, 2):
        to_core(j, p)
    for p in (0, 1):
        for d in (3, 1):
            event(0, d, p)
            event(d, 0, p)
    spread_b(None)
    ahead(j, 2, dev(2, 0))
    event(1, 0, 2)
    event(3, 0, 2)
    for p in (0, 1):
        event(0, 2, p)
        event(2, 0, p)
    event(2, 0, 2)
    for d in (1, 3, 2):
        ahead(j, 2, dev(0, d))
    onward_b(None, 0)
    for dz in (3, 1):
        for dy in (3, 1):
            event(dy, dz, 0)
    partner_b(None)
    for dz in (3, 1):
        for dy in (3, 1):
            event(dy, dz, 1)
    for p in (0, 1):
        for dy in (3, 1):
            event(dy, 2, p)
    onward_b(None, 1)
    for dz in (1, 3, 2):
        event(0, dz, 2)
    last_b(None)
    loads[2].wait()
    for dy in (1, 3):
        for dz in (1, 3, 2):
            event(dy, dz, 2)
    for p in (0, 1):
        for dz in (3, 1):
            event(2, dz, p)
    for p in (0, 1):
        event(2, 2, p)
    for dz in (1, 3, 2):
        event(2, dz, 2)
    for dy in (2, 1, 3, 0):
        first_group(dy)
    square(0)

    def mirror(it, c):
        rows = slice(c * 8, c * 8 + 8)
        arrived(u.at[it, 0:15, rows], u_r.at[it, c])
        for q in range(8):
            xs[it, q, rows] = jnp.concatenate(
                [u[it, i // 2, rows, i % 2 * 192 + q * 24:i % 2 * 192 + q * 24 + 24] for i in range(32)], axis=1)
        for d in (2, 6, 1, 3, 5, 7, 4):
            q = (s + d) % 8
            send(xs.at[it, q, rows], m.at[it, s, rows], m_s.at[it], m_r.at[it, c], (q, t))
        m[it, s, rows] = xs[it, s, rows]

    def update(it, c):
        rows = slice(c * 8, c * 8 + 8)
        arrived(m.at[it, 0:7, rows], m_r.at[it, c])
        tot = ch[...].reshape(8, 24, 768)[:, rows] + m[it, :, rows]
        keep = rowi[:, rows] == coli.reshape(1, 1, 768)
        return jnp.where(keep, -tot / (rowe[:, rows] + cole.reshape(1, 1, 768)), 0.0)

    def next_b(c):
        ball[1, c, s] = update(0, c).reshape(64, 768).astype(BF16)
        spread_b(c)

    mirror(0, 0)
    mirror(0, 1)
    next_b(0)
    mirror(0, 2)
    next_b(1)
    onward_b(0, 0)
    partner_b(0)
    next_b(2)
    onward_b(1, 0, cross=True)
    cross_b(1)
    onward_b(0, 1)
    onward_b(2, 0)
    partner_b(2)
    onward_b(2, 1)
    last_b(0)
    crossed_b(1)
    last_b(2)
    for q in range(8):
        thirds = [ball[1, k, q].astype(F32).reshape(8, 8, 768) for k in range(3)]
        bn[q] = jnp.concatenate([thirds[i % 3][i // 3] for i in range(24)], axis=0).astype(BF16)
    steps = (2, 1, 3, 0)
    product(1, steps[0], second_rhs)
    for g in range(1, 4):
        product(1, steps[g], second_rhs)
        pack(1, steps[g - 1])
        to_mirror(1, steps[g - 1], 0)
    pack(1, steps[3])
    to_mirror(1, steps[3], 0)
    for c in (1, 2):
        for dy in steps:
            to_mirror(1, dy, c)
    square(1)
    for c in range(3):
        mirror(1, c)
    for c in range(3):
        out[:, c * 8:c * 8 + 8] = update(1, c)
    sent(rloc, p_s)
    sent(rsend.at[0:7], a_s)
    sent(rt.at[0:15, :, 0:3072], g_s)
    sent(rt.at[:, :, 0:3072], c_s)
    for it in (0, 1):
        sent(ball.at[it, :, 0:7], b_s.at[it])
        sent(cp.at[it], cp_s.at[it])
        sent(pk.at[it, 0:15], u_s.at[it])
        sent(xs.at[it, 0:7], m_s.at[it])


def local(amplitudes, driving, cycle_ints, occ_irrep, vir_irrep, occ_energy, vir_energy, slab):
    rows, cols = amplitudes.shape
    rloc = cycle_ints.T.reshape(8, 24, cols)
    dma = pltpu.SemaphoreType.DMA
    vmem = pl.BlockSpec(memory_space=pltpu.VMEM)
    result = pl.pallas_call(
        kernel,
        out_shape=jax.ShapeDtypeStruct((8, 24, cols), F32),
        in_specs=[pl.BlockSpec(memory_space=pltpu.HBM)] * 3 + [vmem] * 4 + [pl.BlockSpec(memory_space=pltpu.SMEM)],
        out_specs=vmem,
        scratch_shapes=[
            pltpu.VMEM((192, 768), F32),
            pltpu.VMEM((192, 768), F32),
            pltpu.VMEM((8, 24, 768), BF16),
            pltpu.VMEM((8, 24, 768), BF16),
            pltpu.VMEM((8, 48, 384), BF16),
            pltpu.VMEM((16, 48, 6144), BF16),
            pltpu.VMEM((2, 3, 8, 64, 768), BF16),
            pltpu.VMEM((8, 192, 768), BF16),
            pltpu.VMEM((2, 2, 16, 24, 192), F32),
            pltpu.VMEM((2, 16, 24, 192), F32),
            pltpu.VMEM((2, 16, 24, 384), F32),
            pltpu.VMEM((2, 16, 24, 384), F32),
            pltpu.VMEM((2, 8, 24, 768), F32),
            pltpu.VMEM((2, 8, 24, 768), F32),
            pltpu.VMEM((192, 768), F32),
            dma((3,)), dma, dma, dma, dma, dma, dma((16, 3)), dma, dma((4,)), dma((2,)), dma((8, 2)), dma((3, 8, 2)),
            dma((2,)), dma((2, 4)), dma((2,)), dma((2, 3)), dma((2,)), dma((2, 3)),
        ],
        compiler_params=pltpu.CompilerParams(
            collective_id=0, has_side_effects=True, vmem_limit_bytes=63 * 2**20),
        cost_estimate=pl.CostEstimate(flops=2 * 2 * 192 * 768 * 6144, bytes_accessed=3 * 2**20, transcendentals=0),
    )(amplitudes, driving, rloc, vir_energy.reshape(12, 128), vir_irrep.reshape(12, 128),
      occ_energy.reshape(1, -1), occ_irrep.reshape(1, -1), slab)
    return result.reshape(rows, cols)


def solution(mesh):
    in_specs = (P("ta", "ka"), P("ta", "ka"), P("ka", "ta"), P(), P(), P(), P(), P())
    return jax.shard_map(local, mesh=mesh, in_specs=in_specs, out_specs=P("ta", "ka"), check_vma=False)
```

```python
import jax
import jax.numpy as jnp
from jax import lax
from jax.experimental import pallas as pl
from jax.experimental.pallas import tpu as pltpu
from jax.sharding import PartitionSpec as P

MESH = pl.DeviceIdType.MESH
NT = (((1,), (1,)), ((), ()))
F32, BF16 = jnp.float32, jnp.bfloat16


PIECES = ((0, 1408), (1408, 1280), (2688, 384))


def kernel(amp_h, drv_h, rloc_h, vire, viri, occe, occi, slab, out,
           amp, drv, rloc, rpair, rsend, rt, ball, bn, ct, cp, pk, u, xs, m, ch,
           l_s, p_s, p_r, a_s, a_r, g_s, r_r, c_s, c_r, b_s, b0_r, b1_r, cp_s, cp_r, u_s, u_r, m_s, m_r):
    s = lax.axis_index("ka")
    t = lax.axis_index("ta")
    zlo, x = s // 4, s % 4
    y, zhi, core = t // 8, (t // 2) % 4, t % 2
    j = t // 2
    other = 1 - core

    loads = [pltpu.make_async_copy(rloc_h, rloc, l_s.at[0]),
             pltpu.make_async_copy(amp_h, amp, l_s.at[1]),
             pltpu.make_async_copy(drv_h, drv, l_s.at[2])]
    for copy in loads:
        copy.start()

    def dev(dy, dz):
        return (s, ((y + dy) % 4 * 4 + (zhi + dz) % 4) * 2 + core)

    zp = (1 - zlo) * 4 + x
    cpart = (s, j * 2 + other)
    greet = [dev(0, 1), dev(0, 3), dev(1, 0), dev(3, 0)] + [((s + d) % 8, t) for d in (2, 6, 1, 3, 5, 7, 4)] + [cpart]
    barrier = pltpu.get_barrier_semaphore()
    for peer in greet:
        pl.semaphore_signal(barrier, inc=1, device_id=peer, device_id_type=MESH)
    pl.semaphore_wait(barrier, len(greet))

    def send(src, dst, ss, rs, peer):
        pltpu.make_async_remote_copy(
            src_ref=src, dst_ref=dst, send_sem=ss, recv_sem=rs, device_id=peer, device_id_type=MESH).start()

    def arrived(dst, rs):
        pltpu.make_async_remote_copy(
            src_ref=dst, dst_ref=dst, send_sem=p_s, recv_sem=rs, device_id=cpart, device_id_type=MESH).wait_recv()

    def sent(src, ss):
        pltpu.make_async_remote_copy(
            src_ref=src, dst_ref=src, send_sem=ss, recv_sem=p_r, device_id=cpart, device_id_type=MESH).wait_send()

    loads[0].wait()
    send(rloc, rpair, p_s, p_r, cpart)
    loads[1].wait()
    for k in range(3):
        ball[0, k, s] = amp[k * 64:k * 64 + 64].astype(BF16)
    arrived(rpair, p_r)
    own_first = core == 0
    def kslot(q):
        return pl.ds(pl.multiple_of(core * 3072 + q * 384, 384), 384)

    def both_cores(q):
        a = rloc[q].astype(F32)
        b = rpair[q].astype(F32)
        both = jnp.concatenate([jnp.where(own_first, a, b), jnp.where(own_first, b, a)], axis=0).astype(BF16)
        return jnp.where(own_first, both[:, :384], both[:, 384:])

    for d in (2, 6, 1, 3, 5, 7, 4):
        q = (s + d) % 8
        rsend[q] = both_cores(q)
        send(rsend.at[q], rt.at[j, :, kslot(s)], a_s, a_r, (q, t))
    rt[j, :, kslot(s)] = both_cores(s)

    hot = lax.broadcasted_iota(jnp.int32, (1, 128), 1)

    def slab_at(i):
        here = hot == slab[i]
        return (jnp.sum(jnp.where(here, occe[...], 0.0), axis=1, keepdims=True),
                jnp.sum(jnp.where(here, occi[...], 0), axis=1, keepdims=True))

    def tile_part(v):
        runs = [jnp.concatenate([v[:, i * 192 + q * 24:i * 192 + q * 24 + 24] for i in range(8)], axis=1) for q in range(8)]
        part = runs[0]
        for q in range(1, 8):
            part = jnp.where(s == q, runs[q], part)
        return part

    def row_part(v):
        part = v[:, :192]
        for i in range(1, 8):
            part = jnp.where(t % 8 == i, v[:, i * 192:i * 192 + 192], part)
        return part

    picked = [slab_at(i) for i in range(4)]
    vir_e = jnp.concatenate([vire[i:i + 1] for i in range(12)], axis=1)
    vir_i = jnp.concatenate([viri[i:i + 1] for i in range(12)], axis=1)
    vce, vci = tile_part(vir_e), tile_part(vir_i)
    cole = jnp.concatenate([vce - picked[i][0] for i in range(4)], axis=1)
    coli = jnp.concatenate([jnp.bitwise_xor(vci, picked[i][1]) for i in range(4)], axis=1)
    rowe_v, rowi_v = slab_at(y)
    rowe_l = row_part(vir_e) - rowe_v
    rowi_l = jnp.bitwise_xor(row_part(vir_i), rowi_v).astype(F32)

    def stand(line):
        wide = jnp.concatenate([line, jnp.zeros((1, 64), F32)], axis=1)
        return jnp.broadcast_to(wide, (128, 256)).T[:192, :1]

    rowe = stand(rowe_l).reshape(8, 24, 1)
    rowi = stand(rowi_l).reshape(8, 24, 1)
    coli = coli.astype(F32)

    arrived(rsend.at[0:7], a_r)

    def piece(jj, p, c):
        start, size = PIECES[p]
        return rt.at[jj, :, pl.ds(pl.multiple_of(c * 3072 + start, 128), size)]

    def ahead(jj, p, peer):
        send(piece(jj, p, core), piece(jj, p, core), g_s, r_r.at[jj, p], peer)

    def to_core(jj, p):
        send(piece(jj, p, core), piece(jj, p, core), c_s, c_r.at[jj // 4], cpart)

    def event(dy, dz, p):
        jj = (y + dy) % 4 * 4 + (zhi + dz) % 4
        arrived(piece(jj, p, core), r_r.at[jj, p])
        if p < 2:
            if dy == 0:
                if (dz, p) == (3, 0):
                    ahead(jj, p, dev(0, 1))
                if (dz, p) == (1, 1):
                    ahead(jj, p, dev(0, 3))
                ahead(jj, p, dev(1, 0))
                ahead(jj, p, dev(3, 0))
            if (dy, p) == (3, 0):
                ahead(jj, p, dev(1, 0))
            if (dy, p) == (1, 1):
                ahead(jj, p, dev(3, 0))
        elif dz == 0:
            for d in (1, 3, 2):
                ahead(jj, p, dev(0, d))
        to_core(jj, p)

    def bpart(k, q, h):
        rows = slice(h * 32, h * 32 + 32)
        return (ball.at[0, :, q, rows], b0_r.at[q, h]) if k is None else (ball.at[1, k, q, rows], b1_r.at[k, q, h])

    def b_to(k, q, h, peer):
        ref, sem = bpart(k, q, h)
        send(ref, ref, b_s.at[0 if k is None else 1], sem, (peer, t))

    def b_at(k, q, h):
        arrived(*bpart(k, q, h))

    def round_x(d):
        return zlo * 4 + (x + d) % 4

    def spread_b(k):
        for h in (0, 1):
            b_to(k, s, h, zp)
        for h in (0, 1):
            b_to(k, s, h, round_x(1))
            b_to(k, s, h, round_x(3))

    def partner_b(k):
        for h in (0, 1):
            b_at(k, zp, h)
            b_to(k, zp, h, round_x(1))
            b_to(k, zp, h, round_x(3))

    def onward_b(k, z, cross=False):
        left = (zlo + z) % 2 * 4 + (x + 3) % 4
        right = (zlo + z) % 2 * 4 + (x + 1) % 4
        for q, h in ((left, 0), (right, 1), (left, 1), (right, 0)):
            b_at(k, q, h)
            if (q is left) == (h == 0):
                b_to(k, q, h, round_x(1) if q is left else round_x(3))
            if cross:
                b_to(k, q, h, zp)

    def last_b(k):
        for z in (0, 1):
            for h in (0, 1):
                b_at(k, (zlo + z) % 2 * 4 + (x + 2) % 4, h)

    def cross_b(k):
        for h in (0, 1):
            b_at(k, round_x(2), h)
            b_to(k, round_x(2), h, zp)

    def crossed_b(k):
        for d in range(4):
            for h in (0, 1):
                b_at(k, (1 - zlo) * 4 + (x + d) % 4, h)

    def product(it, dy, rhs):
        yy = (y + dy) % 4
        left = rt[pl.ds(yy * 4, 4)].reshape(192, 6144)
        acc = lax.dot_general(left, rhs(), NT, preferred_element_type=F32).reshape(4, 2, 24, 192)
        ct[it, 0, pl.ds(yy * 4, 4)] = acc[:, 0]
        ct[it, 1, pl.ds(yy * 4, 4)] = acc[:, 1]
        send(ct.at[it, other, pl.ds(yy * 4, 4)], cp.at[it, pl.ds(yy * 4, 4)], cp_s.at[it], cp_r.at[it, yy], cpart)

    def pack(it, dy):
        yy = (y + dy) % 4
        arrived(cp.at[it, pl.ds(yy * 4, 4)], cp_r.at[it, yy])
        for i in range(4):
            mine, theirs = ct[it, core, yy * 4 + i], cp[it, yy * 4 + i]
            pk[it, yy * 4 + i] = jnp.concatenate(
                [jnp.where(own_first, mine, theirs), jnp.where(own_first, theirs, mine)], axis=1)

    def to_mirror(it, dy, c):
        rows = slice(c * 8, c * 8 + 8)
        for dz in (2, 1, 3, 0):
            if dy + dz:
                jj = (y + dy) % 4 * 4 + (zhi + dz) % 4
                send(pk.at[it, jj, rows], u.at[it, j, rows], u_s.at[it], u_r.at[it, c], dev(dy, dz))

    def square(it):
        u[it, j] = pk[it, j]
        c = jnp.concatenate([ct[it, i % 2, i // 2] for i in range(32)], axis=0)
        ch[...] = jnp.concatenate([c, jnp.zeros((768, 64), F32)], axis=1).T[:192] + drv[...]

    def first_rhs():
        return jnp.concatenate([jnp.concatenate([ball[0, k, q, :, h * 384:h * 384 + 384] for k in range(3)], axis=0)
                                for h in (0, 1) for q in range(8)], axis=1)

    def second_rhs():
        return jnp.concatenate([bn[q, :, h * 384:h * 384 + 384] for h in (0, 1) for q in range(8)], axis=1)

    def first_group(dy):
        yy = (y + dy) % 4
        arrived(rt.at[pl.ds(yy * 4, 4), :, pl.ds(pl.multiple_of(other * 3072, 3072), 3072)], c_r.at[yy])
        product(0, dy, first_rhs)
        pack(0, dy)
        for c in range(3):
            to_mirror(0, dy, c)

    for p in (0, 1):
        ahead(j, p, dev(0, 1))
        ahead(j, p, dev(0, 3))
        ahead(j, p, dev(1, 0))
        ahead(j, p, dev(3, 0))
    for d in (1, 3):
        ahead(j, 2, dev(d, 0))
    for p in (0, 1, 2):
        to_core(j, p)
    for p in (0, 1):
        for d in (3, 1):
            event(0, d, p)
            event(d, 0, p)
    spread_b(None)
    ahead(j, 2, dev(2, 0))
    event(1, 0, 2)
    event(3, 0, 2)
    for p in (0, 1):
        event(0, 2, p)
        event(2, 0, p)
    event(2, 0, 2)
    for d in (1, 3, 2):
        ahead(j, 2, dev(0, d))
    onward_b(None, 0)
    for dz in (3, 1):
        for dy in (3, 1):
            event(dy, dz, 0)
    partner_b(None)
    for dz in (3, 1):
        for dy in (3, 1):
            event(dy, dz, 1)
    for p in (0, 1):
        for dy in (3, 1):
            event(dy, 2, p)
    onward_b(None, 1)
    for dz in (1, 3, 2):
        event(0, dz, 2)
    last_b(None)
    loads[2].wait()
    for dy in (1, 3):
        for dz in (1, 3, 2):
            event(dy, dz, 2)
    for p in (0, 1):
        for dz in (3, 1):
            event(2, dz, p)
    for p in (0, 1):
        event(2, 2, p)
    for dz in (1, 3, 2):
        event(2, dz, 2)
    for dy in (2, 1, 3, 0):
        first_group(dy)
    square(0)

    def mirror(it, c):
        rows = slice(c * 8, c * 8 + 8)
        arrived(u.at[it, 0:15, rows], u_r.at[it, c])
        for q in range(8):
            xs[it, q, rows] = jnp.concatenate(
                [u[it, i // 2, rows, i % 2 * 192 + q * 24:i % 2 * 192 + q * 24 + 24] for i in range(32)], axis=1)
        for d in (2, 6, 1, 3, 5, 7, 4):
            q = (s + d) % 8
            send(xs.at[it, q, rows], m.at[it, s, rows], m_s.at[it], m_r.at[it, c], (q, t))
        m[it, s, rows] = xs[it, s, rows]

    def update(it, c):
        rows = slice(c * 8, c * 8 + 8)
        arrived(m.at[it, 0:7, rows], m_r.at[it, c])
        tot = ch[...].reshape(8, 24, 768)[:, rows] + m[it, :, rows]
        keep = rowi[:, rows] == coli.reshape(1, 1, 768)
        return jnp.where(keep, -tot / (rowe[:, rows] + cole.reshape(1, 1, 768)), 0.0)

    def next_b(c):
        ball[1, c, s] = update(0, c).reshape(64, 768).astype(BF16)
        spread_b(c)

    mirror(0, 0)
    mirror(0, 1)
    next_b(0)
    mirror(0, 2)
    next_b(1)
    onward_b(0, 0)
    partner_b(0)
    next_b(2)
    onward_b(1, 0, cross=True)
    cross_b(1)
    onward_b(0, 1)
    onward_b(2, 0)
    partner_b(2)
    onward_b(2, 1)
    last_b(0)
    crossed_b(1)
    last_b(2)
    for q in range(8):
        thirds = [ball[1, k, q].astype(F32).reshape(8, 8, 768) for k in range(3)]
        bn[q] = jnp.concatenate([thirds[i % 3][i // 3] for i in range(24)], axis=0).astype(BF16)
    steps = (2, 1, 3, 0)
    product(1, steps[0], second_rhs)
    for g in range(1, 4):
        product(1, steps[g], second_rhs)
        pack(1, steps[g - 1])
        to_mirror(1, steps[g - 1], 0)
    pack(1, steps[3])
    to_mirror(1, steps[3], 0)
    for c in (1, 2):
        for dy in steps:
            to_mirror(1, dy, c)
    square(1)
    for c in range(3):
        mirror(1, c)
        if c:
            out[:, c * 8 - 8:c * 8] = update(1, c - 1)
    out[:, 16:24] = update(1, 2)
    sent(rloc, p_s)
    sent(rsend.at[0:7], a_s)
    sent(rt.at[0:15, :, 0:3072], g_s)
    sent(rt.at[:, :, 0:3072], c_s)
    for it in (0, 1):
        sent(ball.at[it, :, 0:7], b_s.at[it])
        sent(cp.at[it], cp_s.at[it])
        sent(pk.at[it, 0:15], u_s.at[it])
        sent(xs.at[it, 0:7], m_s.at[it])


def local(amplitudes, driving, cycle_ints, occ_irrep, vir_irrep, occ_energy, vir_energy, slab):
    rows, cols = amplitudes.shape
    rloc = cycle_ints.T.reshape(8, 24, cols)
    dma = pltpu.SemaphoreType.DMA
    vmem = pl.BlockSpec(memory_space=pltpu.VMEM)
    result = pl.pallas_call(
        kernel,
        out_shape=jax.ShapeDtypeStruct((8, 24, cols), F32),
        in_specs=[pl.BlockSpec(memory_space=pltpu.HBM)] * 3 + [vmem] * 4 + [pl.BlockSpec(memory_space=pltpu.SMEM)],
        out_specs=vmem,
        scratch_shapes=[
            pltpu.VMEM((192, 768), F32),
            pltpu.VMEM((192, 768), F32),
            pltpu.VMEM((8, 24, 768), BF16),
            pltpu.VMEM((8, 24, 768), BF16),
            pltpu.VMEM((8, 48, 384), BF16),
            pltpu.VMEM((16, 48, 6144), BF16),
            pltpu.VMEM((2, 3, 8, 64, 768), BF16),
            pltpu.VMEM((8, 192, 768), BF16),
            pltpu.VMEM((2, 2, 16, 24, 192), F32),
            pltpu.VMEM((2, 16, 24, 192), F32),
            pltpu.VMEM((2, 16, 24, 384), F32),
            pltpu.VMEM((2, 16, 24, 384), F32),
            pltpu.VMEM((2, 8, 24, 768), F32),
            pltpu.VMEM((2, 8, 24, 768), F32),
            pltpu.VMEM((192, 768), F32),
            dma((3,)), dma, dma, dma, dma, dma, dma((16, 3)), dma, dma((4,)), dma((2,)), dma((8, 2)), dma((3, 8, 2)),
            dma((2,)), dma((2, 4)), dma((2,)), dma((2, 3)), dma((2,)), dma((2, 3)),
        ],
        compiler_params=pltpu.CompilerParams(
            collective_id=0, has_side_effects=True, vmem_limit_bytes=63 * 2**20),
        cost_estimate=pl.CostEstimate(flops=2 * 2 * 192 * 768 * 6144, bytes_accessed=3 * 2**20, transcendentals=0),
    )(amplitudes, driving, rloc, vir_energy.reshape(12, 128), vir_irrep.reshape(12, 128),
      occ_energy.reshape(1, -1), occ_irrep.reshape(1, -1), slab)
    return result.reshape(rows, cols)


def solution(mesh):
    in_specs = (P("ta", "ka"), P("ta", "ka"), P("ka", "ta"), P(), P(), P(), P(), P())
    return jax.shard_map(local, mesh=mesh, in_specs=in_specs, out_specs=P("ta", "ka"), check_vma=False)
```

```python
import jax
import jax.numpy as jnp
from jax import lax
from jax.experimental import pallas as pl
from jax.experimental.pallas import tpu as pltpu
from jax.sharding import PartitionSpec as P

MESH = pl.DeviceIdType.MESH
NT = (((1,), (1,)), ((), ()))
F32, BF16 = jnp.float32, jnp.bfloat16


PIECES = ((0, 1408), (1408, 1408), (2816, 256))


def kernel(amp_h, drv_h, rloc_h, vire, viri, occe, occi, slab, out,
           amp, drv, rloc, rpair, rsend, rt, ball, bn, ct, cp, pk, u, xs, m, ch,
           l_s, p_s, p_r, a_s, a_r, g_s, r_r, c_s, c_r, b_s, b0_r, b1_r, cp_s, cp_r, u_s, u_r, m_s, m_r):
    s = lax.axis_index("ka")
    t = lax.axis_index("ta")
    zlo, x = s // 4, s % 4
    y, zhi, core = t // 8, (t // 2) % 4, t % 2
    j = t // 2
    other = 1 - core

    loads = [pltpu.make_async_copy(rloc_h, rloc, l_s.at[0]),
             pltpu.make_async_copy(amp_h, amp, l_s.at[1]),
             pltpu.make_async_copy(drv_h, drv, l_s.at[2])]
    for copy in loads:
        copy.start()

    def dev(dy, dz):
        return (s, ((y + dy) % 4 * 4 + (zhi + dz) % 4) * 2 + core)

    zp = (1 - zlo) * 4 + x
    cpart = (s, j * 2 + other)
    greet = [dev(0, 1), dev(0, 3), dev(1, 0), dev(3, 0)] + [((s + d) % 8, t) for d in (2, 6, 1, 3, 5, 7, 4)] + [cpart]
    barrier = pltpu.get_barrier_semaphore()
    for peer in greet:
        pl.semaphore_signal(barrier, inc=1, device_id=peer, device_id_type=MESH)
    pl.semaphore_wait(barrier, len(greet))

    def send(src, dst, ss, rs, peer):
        pltpu.make_async_remote_copy(
            src_ref=src, dst_ref=dst, send_sem=ss, recv_sem=rs, device_id=peer, device_id_type=MESH).start()

    def arrived(dst, rs):
        pltpu.make_async_remote_copy(
            src_ref=dst, dst_ref=dst, send_sem=p_s, recv_sem=rs, device_id=cpart, device_id_type=MESH).wait_recv()

    def sent(src, ss):
        pltpu.make_async_remote_copy(
            src_ref=src, dst_ref=src, send_sem=ss, recv_sem=p_r, device_id=cpart, device_id_type=MESH).wait_send()

    loads[0].wait()
    send(rloc, rpair, p_s, p_r, cpart)
    loads[1].wait()
    for k in range(3):
        ball[0, k, s] = amp[k * 64:k * 64 + 64].astype(BF16)
    arrived(rpair, p_r)
    own_first = core == 0
    for q in range(8):
        a = rloc[q].astype(F32)
        b = rpair[q].astype(F32)
        both = jnp.concatenate([jnp.where(own_first, a, b), jnp.where(own_first, b, a)], axis=0).astype(BF16)
        rsend[q] = jnp.where(own_first, both[:, :384], both[:, 384:])

    def kslot(q):
        return pl.ds(pl.multiple_of(core * 3072 + q * 384, 384), 384)

    for d in range(1, 8):
        q = (s + d) % 8
        send(rsend.at[q], rt.at[j, :, kslot(s)], a_s, a_r, (q, t))
    rt[j, :, kslot(s)] = rsend[s]

    hot = lax.broadcasted_iota(jnp.int32, (1, 128), 1)

    def slab_at(i):
        here = hot == slab[i]
        return (jnp.sum(jnp.where(here, occe[...], 0.0), axis=1, keepdims=True),
                jnp.sum(jnp.where(here, occi[...], 0), axis=1, keepdims=True))

    def tile_part(v):
        runs = [jnp.concatenate([v[:, i * 192 + q * 24:i * 192 + q * 24 + 24] for i in range(8)], axis=1) for q in range(8)]
        part = runs[0]
        for q in range(1, 8):
            part = jnp.where(s == q, runs[q], part)
        return part

    def row_part(v):
        part = v[:, :192]
        for i in range(1, 8):
            part = jnp.where(t % 8 == i, v[:, i * 192:i * 192 + 192], part)
        return part

    picked = [slab_at(i) for i in range(4)]
    vir_e = jnp.concatenate([vire[i:i + 1] for i in range(12)], axis=1)
    vir_i = jnp.concatenate([viri[i:i + 1] for i in range(12)], axis=1)
    vce, vci = tile_part(vir_e), tile_part(vir_i)
    cole = jnp.concatenate([vce - picked[i][0] for i in range(4)], axis=1)
    coli = jnp.concatenate([jnp.bitwise_xor(vci, picked[i][1]) for i in range(4)], axis=1)
    rowe_v, rowi_v = slab_at(y)
    rowe_l = row_part(vir_e) - rowe_v
    rowi_l = jnp.bitwise_xor(row_part(vir_i), rowi_v).astype(F32)

    def stand(line):
        wide = jnp.concatenate([line, jnp.zeros((1, 64), F32)], axis=1)
        return jnp.broadcast_to(wide, (128, 256)).T[:192, :1]

    rowe = stand(rowe_l).reshape(8, 24, 1)
    rowi = stand(rowi_l).reshape(8, 24, 1)
    coli = coli.astype(F32)

    arrived(rsend.at[0:7], a_r)

    def piece(jj, p, c):
        start, size = PIECES[p]
        return rt.at[jj, :, pl.ds(pl.multiple_of(c * 3072 + start, 128), size)]

    def ahead(jj, p, peer):
        send(piece(jj, p, core), piece(jj, p, core), g_s, r_r.at[jj, p], peer)

    def to_core(jj, p):
        send(piece(jj, p, core), piece(jj, p, core), c_s, c_r.at[jj // 4], cpart)

    def event(dy, dz, p):
        jj = (y + dy) % 4 * 4 + (zhi + dz) % 4
        arrived(piece(jj, p, core), r_r.at[jj, p])
        if p < 2:
            if dy == 0:
                if (dz, p) == (3, 0):
                    ahead(jj, p, dev(0, 1))
                if (dz, p) == (1, 1):
                    ahead(jj, p, dev(0, 3))
                ahead(jj, p, dev(1, 0))
                ahead(jj, p, dev(3, 0))
            if (dy, p) == (3, 0):
                ahead(jj, p, dev(1, 0))
            if (dy, p) == (1, 1):
                ahead(jj, p, dev(3, 0))
        elif dz == 0:
            for d in (1, 3, 2):
                ahead(jj, p, dev(0, d))
        to_core(jj, p)

    def bpart(k, q, h):
        rows = slice(h * 32, h * 32 + 32)
        return (ball.at[0, :, q, rows], b0_r.at[q, h]) if k is None else (ball.at[1, k, q, rows], b1_r.at[k, q, h])

    def b_to(k, q, h, peer):
        ref, sem = bpart(k, q, h)
        send(ref, ref, b_s.at[0 if k is None else 1], sem, (peer, t))

    def b_at(k, q, h):
        arrived(*bpart(k, q, h))

    def round_x(d):
        return zlo * 4 + (x + d) % 4

    def spread_b(k):
        for h in (0, 1):
            b_to(k, s, h, zp)
        for h in (0, 1):
            b_to(k, s, h, round_x(1))
            b_to(k, s, h, round_x(3))

    def partner_b(k):
        for h in (0, 1):
            b_at(k, zp, h)
            b_to(k, zp, h, round_x(1))
            b_to(k, zp, h, round_x(3))

    def onward_b(k, z, cross=False):
        left = (zlo + z) % 2 * 4 + (x + 3) % 4
        right = (zlo + z) % 2 * 4 + (x + 1) % 4
        for q, h in ((left, 0), (right, 1), (left, 1), (right, 0)):
            b_at(k, q, h)
            if (q is left) == (h == 0):
                b_to(k, q, h, round_x(1) if q is left else round_x(3))
            if cross:
                b_to(k, q, h, zp)

    def last_b(k):
        for z in (0, 1):
            for h in (0, 1):
                b_at(k, (zlo + z) % 2 * 4 + (x + 2) % 4, h)

    def cross_b(k):
        for h in (0, 1):
            b_at(k, round_x(2), h)
            b_to(k, round_x(2), h, zp)

    def crossed_b(k):
        for d in range(4):
            for h in (0, 1):
                b_at(k, (1 - zlo) * 4 + (x + d) % 4, h)

    def product(it, dy, rhs):
        yy = (y + dy) % 4
        left = rt[pl.ds(yy * 4, 4)].reshape(192, 6144)
        acc = lax.dot_general(left, rhs(), NT, preferred_element_type=F32).reshape(4, 2, 24, 192)
        ct[it, 0, pl.ds(yy * 4, 4)] = acc[:, 0]
        ct[it, 1, pl.ds(yy * 4, 4)] = acc[:, 1]
        send(ct.at[it, other, pl.ds(yy * 4, 4)], cp.at[it, pl.ds(yy * 4, 4)], cp_s.at[it], cp_r.at[it, yy], cpart)

    def pack(it, dy):
        yy = (y + dy) % 4
        arrived(cp.at[it, pl.ds(yy * 4, 4)], cp_r.at[it, yy])
        for i in range(4):
            mine, theirs = ct[it, core, yy * 4 + i], cp[it, yy * 4 + i]
            pk[it, yy * 4 + i] = jnp.concatenate(
                [jnp.where(own_first, mine, theirs), jnp.where(own_first, theirs, mine)], axis=1)

    def to_mirror(it, dy, c):
        rows = slice(c * 8, c * 8 + 8)
        for dz in (2, 1, 3, 0):
            if dy + dz:
                jj = (y + dy) % 4 * 4 + (zhi + dz) % 4
                send(pk.at[it, jj, rows], u.at[it, j, rows], u_s.at[it], u_r.at[it, c], dev(dy, dz))

    def square(it):
        u[it, j] = pk[it, j]
        c = jnp.concatenate([ct[it, i % 2, i // 2] for i in range(32)], axis=0)
        ch[...] = jnp.concatenate([c, jnp.zeros((768, 64), F32)], axis=1).T[:192] + drv[...]

    def first_rhs():
        return jnp.concatenate([jnp.concatenate([ball[0, k, q, :, h * 384:h * 384 + 384] for k in range(3)], axis=0)
                                for h in (0, 1) for q in range(8)], axis=1)

    def second_rhs():
        return jnp.concatenate([bn[q, :, h * 384:h * 384 + 384] for h in (0, 1) for q in range(8)], axis=1)

    def first_group(dy):
        yy = (y + dy) % 4
        arrived(rt.at[pl.ds(yy * 4, 4), :, pl.ds(pl.multiple_of(other * 3072, 3072), 3072)], c_r.at[yy])
        product(0, dy, first_rhs)
        pack(0, dy)
        for c in range(3):
            to_mirror(0, dy, c)

    for p in (0, 1):
        ahead(j, p, dev(0, 1))
        ahead(j, p, dev(0, 3))
        ahead(j, p, dev(1, 0))
        ahead(j, p, dev(3, 0))
    for d in (1, 3):
        ahead(j, 2, dev(d, 0))
    for p in (0, 1, 2):
        to_core(j, p)
    for p in (0, 1):
        for d in (3, 1):
            event(0, d, p)
            event(d, 0, p)
    spread_b(None)
    ahead(j, 2, dev(2, 0))
    event(1, 0, 2)
    event(3, 0, 2)
    for p in (0, 1):
        event(0, 2, p)
        event(2, 0, p)
    event(2, 0, 2)
    for d in (1, 3, 2):
        ahead(j, 2, dev(0, d))
    onward_b(None, 0)
    for dz in (3, 1):
        for dy in (3, 1):
            event(dy, dz, 0)
    partner_b(None)
    for dz in (3, 1):
        for dy in (3, 1):
            event(dy, dz, 1)
    for p in (0, 1):
        for dy in (3, 1):
            event(dy, 2, p)
    onward_b(None, 1)
    for dz in (1, 3, 2):
        event(0, dz, 2)
    last_b(None)
    loads[2].wait()
    for dy in (1, 3):
        for dz in (1, 3, 2):
            event(dy, dz, 2)
    for p in (0, 1):
        for dz in (3, 1):
            event(2, dz, p)
    for p in (0, 1):
        event(2, 2, p)
    for dz in (1, 3, 2):
        event(2, dz, 2)
    for dy in (2, 1, 3, 0):
        first_group(dy)
    square(0)

    def mirror(it, c):
        rows = slice(c * 8, c * 8 + 8)
        arrived(u.at[it, 0:15, rows], u_r.at[it, c])
        for q in range(8):
            xs[it, q, rows] = jnp.concatenate(
                [u[it, i // 2, rows, i % 2 * 192 + q * 24:i % 2 * 192 + q * 24 + 24] for i in range(32)], axis=1)
        for d in (2, 6, 1, 3, 5, 7, 4):
            q = (s + d) % 8
            send(xs.at[it, q, rows], m.at[it, s, rows], m_s.at[it], m_r.at[it, c], (q, t))
        m[it, s, rows] = xs[it, s, rows]

    def update(it, c):
        rows = slice(c * 8, c * 8 + 8)
        arrived(m.at[it, 0:7, rows], m_r.at[it, c])
        tot = ch[...].reshape(8, 24, 768)[:, rows] + m[it, :, rows]
        keep = rowi[:, rows] == coli.reshape(1, 1, 768)
        return jnp.where(keep, -tot / (rowe[:, rows] + cole.reshape(1, 1, 768)), 0.0)

    def next_b(c):
        ball[1, c, s] = update(0, c).reshape(64, 768).astype(BF16)
        spread_b(c)

    mirror(0, 0)
    mirror(0, 1)
    next_b(0)
    mirror(0, 2)
    next_b(1)
    onward_b(0, 0)
    partner_b(0)
    next_b(2)
    onward_b(1, 0, cross=True)
    cross_b(1)
    onward_b(0, 1)
    onward_b(2, 0)
    partner_b(2)
    onward_b(2, 1)
    last_b(0)
    crossed_b(1)
    last_b(2)
    for q in range(8):
        thirds = [ball[1, k, q].astype(F32).reshape(8, 8, 768) for k in range(3)]
        bn[q] = jnp.concatenate([thirds[i % 3][i // 3] for i in range(24)], axis=0).astype(BF16)
    steps = (2, 1, 3, 0)
    product(1, steps[0], second_rhs)
    for g in range(1, 4):
        product(1, steps[g], second_rhs)
        pack(1, steps[g - 1])
        to_mirror(1, steps[g - 1], 0)
    pack(1, steps[3])
    to_mirror(1, steps[3], 0)
    for c in (1, 2):
        for dy in steps:
            to_mirror(1, dy, c)
    square(1)
    for c in range(3):
        mirror(1, c)
    for c in range(3):
        out[:, c * 8:c * 8 + 8] = update(1, c)
    sent(rloc, p_s)
    sent(rsend.at[0:7], a_s)
    sent(rt.at[0:15, :, 0:3072], g_s)
    sent(rt.at[:, :, 0:3072], c_s)
    for it in (0, 1):
        sent(ball.at[it, :, 0:7], b_s.at[it])
        sent(cp.at[it], cp_s.at[it])
        sent(pk.at[it, 0:15], u_s.at[it])
        sent(xs.at[it, 0:7], m_s.at[it])


def local(amplitudes, driving, cycle_ints, occ_irrep, vir_irrep, occ_energy, vir_energy, slab):
    rows, cols = amplitudes.shape
    rloc = cycle_ints.T.reshape(8, 24, cols)
    dma = pltpu.SemaphoreType.DMA
    vmem = pl.BlockSpec(memory_space=pltpu.VMEM)
    result = pl.pallas_call(
        kernel,
        out_shape=jax.ShapeDtypeStruct((8, 24, cols), F32),
        in_specs=[pl.BlockSpec(memory_space=pltpu.HBM)] * 3 + [vmem] * 4 + [pl.BlockSpec(memory_space=pltpu.SMEM)],
        out_specs=vmem,
        scratch_shapes=[
            pltpu.VMEM((192, 768), F32),
            pltpu.VMEM((192, 768), F32),
            pltpu.VMEM((8, 24, 768), BF16),
            pltpu.VMEM((8, 24, 768), BF16),
            pltpu.VMEM((8, 48, 384), BF16),
            pltpu.VMEM((16, 48, 6144), BF16),
            pltpu.VMEM((2, 3, 8, 64, 768), BF16),
            pltpu.VMEM((8, 192, 768), BF16),
            pltpu.VMEM((2, 2, 16, 24, 192), F32),
            pltpu.VMEM((2, 16, 24, 192), F32),
            pltpu.VMEM((2, 16, 24, 384), F32),
            pltpu.VMEM((2, 16, 24, 384), F32),
            pltpu.VMEM((2, 8, 24, 768), F32),
            pltpu.VMEM((2, 8, 24, 768), F32),
            pltpu.VMEM((192, 768), F32),
            dma((3,)), dma, dma, dma, dma, dma, dma((16, 3)), dma, dma((4,)), dma((2,)), dma((8, 2)), dma((3, 8, 2)),
            dma((2,)), dma((2, 4)), dma((2,)), dma((2, 3)), dma((2,)), dma((2, 3)),
        ],
        compiler_params=pltpu.CompilerParams(
            collective_id=0, has_side_effects=True, vmem_limit_bytes=63 * 2**20),
        cost_estimate=pl.CostEstimate(flops=2 * 2 * 192 * 768 * 6144, bytes_accessed=3 * 2**20, transcendentals=0),
    )(amplitudes, driving, rloc, vir_energy.reshape(12, 128), vir_irrep.reshape(12, 128),
      occ_energy.reshape(1, -1), occ_irrep.reshape(1, -1), slab)
    return result.reshape(rows, cols)


def solution(mesh):
    in_specs = (P("ta", "ka"), P("ta", "ka"), P("ka", "ta"), P(), P(), P(), P(), P())
    return jax.shard_map(local, mesh=mesh, in_specs=in_specs, out_specs=P("ta", "ka"), check_vma=False)
```
